128 devices in a mesh: dp: 4 (over x), slab: 32 (over z, y, core).
Axes of the slice: x: 4, y: 4, z: 4, core: 2. Of those that a mesh axis runs over, the one named last changes fastest.
Arguments:
- features: bfloat16 [4, 32, 4, 16, 16, 1024], P('dp', 'slab'), may hold values from -6 to 6
- target: float32 [4, 32, 4, 16, 256], P('dp', 'slab'), may hold values from -6 to 6
- block_coords: int32 [4, 32, 4, 2], P('dp', 'slab'), may hold values from -1 to 15, as said below
- neighbours: int32 [4, 32, 4, 6], P('dp', 'slab'), may hold values from -1 to 3, as said below
- owners: int32 [4, 32, 4, 2], P('dp', 'slab'), may hold values from -1 to 31, as said below
- coarse_weight: bfloat16 [27, 4096], replicated, may hold values from -0.15625 to 0.15625
- decoder_weight: bfloat16 [27, 64], replicated, may hold values from -0.15625 to 0.15625
Outputs:
- residual: float32 [4, 32, 4, 16, 256], P('dp', 'slab')
- grad_coarse: float32 [27, 4096], P(None, 'slab')
- grad_decoder: float32 [27, 64], replicated
The draws below stay inside these ranges and needn't reach their ends.
Inputs may be any that keep to these rules, and one draw needn't show every extreme that they name: `block_coords`: for an occupied slot the (x, y) block position on a 16 x 16 grid of the slab, distinct within a slab; (-1, -1) marks an empty slot. Empty slots lie anywhere in the list; in every draw some slab's list has no empty slot. In every tomogram one block position is occupied in every slab. `neighbours`: for an occupied slot of slab s, the list slots of the occupied blocks sharing its -z face (in slab s - 1, same position), +z face (in slab s + 1), and its -y, +y, -x, +x faces (in slab s, position changed by one); -1 where there is no such block, and all -1 for an empty slot. The relation is symmetric and agrees with block_coords. `owners`: A coarse block covers 2 x 2 fine block positions in x and y over the slabs 2j and 2j + 1 of a tomogram; an occupied fine block names (owner slab, owner slot) of its coarse block, the owner being a slab of the same tomogram. All fine blocks of a coarse block name the same pair, no two coarse blocks do, and each slab of a tomogram owns exactly 1 coarse blocks, in slots 0 to 0. One slab names one owner at most 2 times, and some slab names some owner exactly 2 times. (-1, -1) for an empty slot.
All inputs are finite; a program needn't handle non-finite values.
Results may differ from the reference program's by a relative error of at most 0.003.
The reference program's roundings to bfloat16 on the way count: a program that leaves them out, or rounds other values in their place, can miss the bound.
Values may be sent and summed in bfloat16 or wider, within the bound.
A program may use at most 192 MiB of HBM per device.

```python
import jax
import jax.numpy as jnp
from jax import lax

CHANNELS = 64
EDGE = 16
GRID = 16
CCAP = 1
BLK = 4
VOLUMES = 4
SLABS = 32
CELLS = 16384


def distinct_order(key, shape):
    length = shape[-1]
    scores = jax.random.randint(key, shape, 0, 1 << 12) * length + jnp.arange(length, dtype=jnp.int32)
    return jnp.argsort(scores, axis=-1)


def locate(target_x, target_y, list_x, list_y, list_live):
    match = (target_x[:, :, None] == list_x[:, None, :]) & (target_y[:, :, None] == list_y[:, None, :]) & list_live[:, None, :]
    found = jnp.sum(jnp.where(match, jnp.arange(BLK, dtype=jnp.int32)[None, None, :], 0), axis=-1)
    return jnp.where(jnp.any(match, axis=-1), found, -1)


def volume_layout(key):
    pairs = SLABS // 2
    most = 4 * CCAP
    half_grid = GRID // 2
    keys = jax.random.split(key, 8)
    common_place = jax.random.randint(jax.random.fold_in(key, 11), (), 0, half_grid * half_grid)
    common_quad = jax.random.randint(jax.random.fold_in(key, 12), (), 0, 4)
    owner_rank = jax.random.permutation(keys[0], SLABS)
    rank_owner = jnp.argsort(owner_rank).astype(jnp.int32)
    quarter = pairs // 4
    levels = jnp.concatenate([jnp.full((quarter,), 4 * CCAP, jnp.int32), jnp.full((quarter,), 2 * CCAP, jnp.int32), jnp.full((pairs - 2 * quarter,), CCAP, jnp.int32)])
    lengths = jax.random.permutation(keys[1], levels)
    starts = jnp.cumsum(lengths) - lengths
    heavy = (lengths == 4 * CCAP).astype(jnp.int32)
    medium = (lengths == 2 * CCAP).astype(jnp.int32)
    pick_scores = jax.random.randint(keys[2], (2, pairs), 0, 1 << 12) * pairs + jnp.arange(pairs, dtype=jnp.int32)
    heavy_pick = jnp.argsort(-(pick_scores[0] + heavy * (1 << 24)))[0]
    medium_pick = jnp.argsort(-(pick_scores[1] + medium * (1 << 24)))[0]
    raw_counts = jax.random.randint(keys[3], (pairs, most, 2), 0, 6)
    counts = jnp.where(heavy[:, None, None] == 1, jnp.minimum(raw_counts, 1), jnp.minimum((raw_counts + 1) // 2, 2))
    nothing = counts[..., 0] + counts[..., 1] == 0
    counts = jnp.stack([jnp.where(nothing, 1, counts[..., 0]), counts[..., 1]], axis=-1)
    pair_ids = jnp.arange(pairs, dtype=jnp.int32)[:, None, None]
    half_ids = jnp.arange(2, dtype=jnp.int32)[None, None, :]
    counts = jnp.where(pair_ids == heavy_pick, 1, counts)
    counts = jnp.where((pair_ids == medium_pick) & (half_ids == 0), 2, counts)
    first_coarse = jnp.arange(most, dtype=jnp.int32)[None, :, None] == 0
    counts = jnp.where(first_coarse, jnp.maximum(counts, 1), counts)
    exists = jnp.arange(most, dtype=jnp.int32)[None, :] < lengths[:, None]
    counts = jnp.where(exists[:, :, None], counts, 0)
    place_range = jnp.arange(half_grid * half_grid, dtype=jnp.int32)
    place_scores = jax.random.randint(keys[4], (pairs, half_grid * half_grid), 0, 1 << 12) * (half_grid * half_grid) + place_range
    place_scores = jnp.where(place_range[None, :] == common_place, -1, place_scores)
    place_order = jnp.argsort(place_scores, axis=-1)[:, :most]
    quad_range = jnp.arange(4, dtype=jnp.int32)
    quad_scores = jax.random.randint(keys[5], (pairs, most, 2, 4), 0, 1 << 12) * 4 + quad_range
    force_quad = (jnp.arange(most, dtype=jnp.int32)[None, :, None, None] == 0) & (quad_range[None, None, None, :] == common_quad)
    quad_scores = jnp.where(force_quad, -1, quad_scores)
    quads = jnp.argsort(quad_scores, axis=-1)[..., :2]
    slot_t = starts[:, None] + jnp.arange(most, dtype=jnp.int32)[None, :]
    owner_of = rank_owner[slot_t % SLABS]
    slot_of = slot_t // SLABS
    coarse_x = place_order % half_grid
    coarse_y = place_order // half_grid
    block_x = 2 * coarse_x[:, :, None, None] + quads % 2
    block_y = 2 * coarse_y[:, :, None, None] + quads // 2
    live = jnp.arange(2, dtype=jnp.int32)[None, None, None, :] < counts[:, :, :, None]
    full_shape = (pairs, most, 2, 2)

    def arrange(values):
        return jnp.transpose(jnp.broadcast_to(values, full_shape), (0, 2, 1, 3)).reshape(pairs, 2, most * 2)
    live_c = arrange(live)
    x_c = arrange(block_x)
    y_c = arrange(block_y)
    owner_c = arrange(owner_of[:, :, None, None])
    slot_c = arrange(slot_of[:, :, None, None])
    scores = (1 - live_c.astype(jnp.int32)) * (1 << 24) + jax.random.randint(keys[6], (pairs, 2, most * 2), 0, 1 << 12) * (most * 2) + jnp.arange(most * 2, dtype=jnp.int32)
    chosen = jnp.argsort(scores, axis=-1)[..., :BLK]
    chosen = jnp.take_along_axis(chosen, distinct_order(keys[7], (pairs, 2, BLK)), axis=-1)

    def select(values):
        return jnp.take_along_axis(values, chosen, axis=-1).reshape(SLABS, BLK)
    live_s = select(live_c)
    x_s = jnp.where(live_s, select(x_c), -1)
    y_s = jnp.where(live_s, select(y_c), -1)
    owner_s = jnp.where(live_s, select(owner_c), -1)
    slot_s = jnp.where(live_s, select(slot_c), -1)
    empty_row = jnp.full((1, BLK), -1, jnp.int32)
    dead_row = jnp.zeros((1, BLK), bool)
    lower_x = jnp.concatenate([empty_row, x_s[:-1]], axis=0)
    lower_y = jnp.concatenate([empty_row, y_s[:-1]], axis=0)
    lower_live = jnp.concatenate([dead_row, live_s[:-1]], axis=0)
    upper_x = jnp.concatenate([x_s[1:], empty_row], axis=0)
    upper_y = jnp.concatenate([y_s[1:], empty_row], axis=0)
    upper_live = jnp.concatenate([live_s[1:], dead_row], axis=0)
    links = jnp.stack([locate(x_s, y_s, lower_x, lower_y, lower_live), locate(x_s, y_s, upper_x, upper_y, upper_live), locate(x_s, y_s - 1, x_s, y_s, live_s), locate(x_s, y_s + 1, x_s, y_s, live_s), locate(x_s - 1, y_s, x_s, y_s, live_s), locate(x_s + 1, y_s, x_s, y_s, live_s)], axis=-1)
    links = jnp.where(live_s[..., None], links, -1)
    coords = jnp.stack([x_s, y_s], axis=-1)
    owner_pairs = jnp.stack([owner_s, slot_s], axis=-1)
    return (coords.astype(jnp.int32), links.astype(jnp.int32), owner_pairs.astype(jnp.int32))


def build_layout(key):
    base_key = jax.random.fold_in(key, 7)
    volume_keys = jax.vmap(lambda volume: jax.random.fold_in(base_key, volume))(jnp.arange(VOLUMES, dtype=jnp.int32))
    return jax.vmap(volume_layout)(volume_keys)


def draw_block_coords(key, part):
    return build_layout(key)[0]


def draw_neighbours(key, part):
    return build_layout(key)[1]


def draw_owners(key, part):
    return build_layout(key)[2]


def block_scale(stream_key, extent, cuts, least, top_value):
    factor_of = 1.0
    for axis_at, blocks in cuts:
        steps = jax.random.uniform(jax.random.fold_in(jax.random.fold_in(stream_key, 6), axis_at), (blocks,), jnp.float32, least / len(cuts), top_value / len(cuts))
        factor_of = factor_of * jnp.repeat(jnp.exp(steps), extent[axis_at] // blocks).reshape((-1,) + (1,) * (len(extent) - 1 - axis_at))
    return factor_of


def normal_values(key, dims, scale, most, cuts=(), held_as=jnp.bfloat16):
    entries = scale * jax.random.normal(key, dims, jnp.float32)
    if cuts:
        entries = entries * block_scale(key, dims, cuts, -0.22, 0.18)
    return jnp.clip(entries, -most, most).astype(held_as)


def setup_inputs(seed: int = 0) -> dict:
    splits = jax.random.split(jax.random.key(seed), 8)
    return {
        "features": normal_values(splits[0], (VOLUMES, SLABS, BLK, EDGE, EDGE, EDGE * CHANNELS), 1.0, 6.0, ((0, 4), (1, 32))),
        "target": normal_values(splits[1], (VOLUMES, SLABS, BLK, EDGE, EDGE * EDGE), 1.0, 6.0, ((0, 4), (1, 32)), jnp.float32),
        "block_coords": draw_block_coords(jax.random.fold_in(splits[7], 71), 0),
        "neighbours": draw_neighbours(jax.random.fold_in(splits[7], 71), 0),
        "owners": draw_owners(jax.random.fold_in(splits[7], 71), 0),
        "coarse_weight": normal_values(splits[5], (27, CHANNELS * CHANNELS), (27 * CHANNELS) ** -0.5, 0.15625),
        "decoder_weight": normal_values(splits[6], (27, CHANNELS), (27 * CHANNELS) ** -0.5, 0.15625),
    }


def offset_list():
    triples = []
    for step_z in range(3):
        for step_y in range(3):
            for step_x in range(3):
                triples.append((step_z, step_y, step_x))
    return triples

def take_planes(planes, picked):
    safe_index = jnp.maximum(picked, 0)
    fetched = jnp.take(planes, safe_index, axis=0)
    keep_mask = (picked >= 0).reshape((-1,) + (1,) * (planes.ndim - 1))
    return jnp.where(keep_mask, fetched, jnp.zeros_like(fetched))

def frame_blocks(volume, below_rim, above_rim, link_ids, plane_width):
    sectioned = jnp.concatenate([take_planes(below_rim, link_ids[:, 0])[:, None], volume, take_planes(above_rim, link_ids[:, 1])[:, None]], axis=1)
    lower_side = take_planes(sectioned[:, :, -1], link_ids[:, 2])
    upper_side = take_planes(sectioned[:, :, 0], link_ids[:, 3])
    sectioned = jnp.concatenate([lower_side[:, :, None], sectioned, upper_side[:, :, None]], axis=2)
    lower_side = take_planes(sectioned[:, :, :, -plane_width:], link_ids[:, 4])
    upper_side = take_planes(sectioned[:, :, :, :plane_width], link_ids[:, 5])
    return jnp.concatenate([lower_side, sectioned, upper_side], axis=3)

def pool_mean(values, half_edge, channels):
    count_blocks = values.shape[0]
    grouped = values.astype(jnp.float32).reshape(count_blocks, half_edge, 2, half_edge, 2, half_edge, 2, channels)
    return grouped.mean(axis=(2, 4, 6)).reshape(count_blocks, half_edge, half_edge, half_edge * channels)

def pool_sum(values, count_blocks, half_edge, channels):
    grouped = values.reshape(count_blocks, half_edge, 2, half_edge, 2, half_edge, 2, channels)
    return grouped.sum(axis=(2, 4, 6)).reshape(count_blocks, half_edge, half_edge, half_edge * channels)

def upsample(octants, half_edge, channels):
    count_blocks = octants.shape[0]
    expanded = jnp.broadcast_to(octants.reshape(count_blocks, half_edge, 1, half_edge, 1, half_edge, 1, channels), (count_blocks, half_edge, 2, half_edge, 2, half_edge, 2, channels))
    return expanded.reshape(count_blocks, 2 * half_edge, 2 * half_edge, 2 * half_edge * channels)

def octants_to_blocks(octants, count_coarse, half_edge, channels):
    grouped = octants.reshape(count_coarse, 2, 2, 2, half_edge, half_edge, half_edge, channels)
    return grouped.transpose(0, 1, 4, 2, 5, 3, 6, 7).reshape(count_coarse, 2 * half_edge, 2 * half_edge, 2 * half_edge * channels)

def blocks_to_octants(blocks, half_edge, channels):
    count_coarse = blocks.shape[0]
    grouped = blocks.reshape(count_coarse, 2, half_edge, 2, half_edge, 2, half_edge, channels)
    return grouped.transpose(0, 1, 3, 5, 2, 4, 6, 7).reshape(count_coarse * 8, half_edge, half_edge, half_edge * channels)

def coarse_patch(framed, step_z, step_y, block_edge, channels):
    window = framed[:, step_z:step_z + block_edge, step_y:step_y + block_edge, :]
    pieces = [window[..., step_x * channels:(step_x + block_edge) * channels].reshape(-1, channels) for step_x in range(3)]
    return jnp.concatenate(pieces, axis=1).astype(jnp.float32)

def coarse_forward(framed, kernel_rows, block_edge, channels):
    summed = jnp.zeros((framed.shape[0] * block_edge ** 3, channels), jnp.float32)
    for step_z in range(3):
        for step_y in range(3):
            patch = coarse_patch(framed, step_z, step_y, block_edge, channels)
            summed = summed + jnp.dot(patch, kernel_rows[3 * step_z + step_y].astype(jnp.float32), preferred_element_type=jnp.float32)
    return summed

def coarse_kernel_grad(framed, cotangent, block_edge, channels):
    terms = []
    for step_z in range(3):
        for step_y in range(3):
            patch = coarse_patch(framed, step_z, step_y, block_edge, channels)
            terms.append(lax.dot_general(patch, cotangent.astype(jnp.float32), (((0,), (0,)), ((), ())), preferred_element_type=jnp.float32))
    return jnp.stack(terms)

def decode(framed, kernel, block_edge, channels):
    count_blocks = framed.shape[0]
    flattened = framed.reshape(-1, channels).astype(jnp.float32)
    projected = lax.dot_general(kernel.astype(jnp.float32), flattened, (((1,), (1,)), ((), ())), preferred_element_type=jnp.float32)
    projected = projected.reshape(27, count_blocks, block_edge + 2, block_edge + 2, block_edge + 2)
    summed = jnp.zeros((count_blocks, block_edge, block_edge, block_edge), jnp.float32)
    for position, (step_z, step_y, step_x) in enumerate(offset_list()):
        summed = summed + projected[position, :, step_z:step_z + block_edge, step_y:step_y + block_edge, step_x:step_x + block_edge]
    return summed

def kernel_term(framed, cotangent, channels):
    shifted = jnp.stack([jnp.pad(cotangent, ((0, 0), (step_z, 2 - step_z), (step_y, 2 - step_y), (step_x, 2 - step_x))) for step_z, step_y, step_x in offset_list()])
    return jnp.dot(shifted.reshape(27, -1).astype(jnp.float32), framed.reshape(-1, channels).astype(jnp.float32), preferred_element_type=jnp.float32)

def spread(framed_cot, kernel, block_edge):
    taps = jnp.stack([framed_cot[:, 2 - step_z:2 - step_z + block_edge, 2 - step_y:2 - step_y + block_edge, 2 - step_x:2 - step_x + block_edge] for step_z, step_y, step_x in offset_list()])
    return lax.dot_general(taps.reshape(27, -1).astype(jnp.float32), kernel.astype(jnp.float32), (((0,), (0,)), ((), ())), preferred_element_type=jnp.float32)

def neighbour_planes(field, first_plane, last_plane):
    zero_plane = jnp.zeros_like(last_plane[:, :1])
    below_rim = jnp.concatenate([zero_plane, last_plane[:, :-1]], axis=1)
    above_rim = jnp.concatenate([first_plane[:, 1:], zero_plane], axis=1)
    return (below_rim, above_rim)

def reference(features, target, block_coords, neighbours, owners, coarse_weight, decoder_weight):
    block_edge = EDGE
    channels = CHANNELS
    half_edge = EDGE // 2
    slab_total = VOLUMES * SLABS
    live_slot = owners[..., 0] >= 0
    flat_live = live_slot.reshape(slab_total, BLK)
    fine_all = features.reshape(slab_total, BLK, block_edge, block_edge, block_edge * channels)

    def pool_slab(packed):
        fine_feat, live_here = packed
        pooled_here = jnp.where(live_here[:, None, None, None], pool_mean(fine_feat, half_edge, channels), 0.0)
        return pooled_here.astype(jnp.bfloat16)
    pooled = lax.map(pool_slab, (fine_all, flat_live))
    half_of_slab = (jnp.arange(SLABS, dtype=jnp.int32) % 2)[None, :, None]
    octant_code = owners[..., 1] * 8 + half_of_slab * 4 + block_coords[..., 1] % 2 * 2 + block_coords[..., 0] % 2
    volume_ids = jnp.arange(VOLUMES, dtype=jnp.int32)[:, None, None]
    octant_total = slab_total * CCAP * 8
    target_row = (volume_ids * SLABS + owners[..., 0]) * (CCAP * 8) + octant_code
    target_row = jnp.where(live_slot, target_row, octant_total).reshape(-1).astype(jnp.int32)
    octant_shape = (half_edge, half_edge, half_edge * channels)
    coarse_oct = jnp.zeros((octant_total,) + octant_shape, jnp.bfloat16).at[target_row].set(pooled.reshape((-1,) + octant_shape), mode='drop')
    coarse_in = octants_to_blocks(coarse_oct, slab_total * CCAP, half_edge, channels)
    kernel_rows = coarse_weight.reshape(9, 3 * channels, channels)

    def coarse_one(block):
        framed = jnp.pad(block[None], ((0, 0), (1, 1), (1, 1), (channels, channels)))
        pre_act = coarse_forward(framed, kernel_rows, block_edge, channels)
        activated = jnp.maximum(pre_act, 0.0).astype(jnp.bfloat16).reshape(block_edge, block_edge, block_edge * channels)
        return (activated, pre_act > 0)
    coarse_out, coarse_active = lax.map(coarse_one, coarse_in)
    back_oct = blocks_to_octants(coarse_out, half_edge, channels)
    upward = jnp.take(back_oct, jnp.minimum(target_row, octant_total - 1), axis=0).reshape((slab_total, BLK) + octant_shape)

    def mix_slab(packed):
        fine_feat, up_here, live_here = packed
        summed = fine_feat.astype(jnp.float32) + upsample(up_here, half_edge, channels).astype(jnp.float32)
        return jnp.where(live_here[:, None, None, None], summed, 0.0).astype(jnp.bfloat16)
    mixed = lax.map(mix_slab, (fine_all, upward, flat_live))
    mixed_grid = mixed.reshape(VOLUMES, SLABS, BLK, block_edge, block_edge, block_edge * channels)
    below_rim, above_rim = neighbour_planes(mixed_grid, mixed_grid[:, :, :, 0], mixed_grid[:, :, :, -1])
    plane_shape = (BLK, block_edge, block_edge * channels)
    link_all = neighbours.reshape(slab_total, BLK, 6)
    measured_all = target.reshape(slab_total, BLK, block_edge, block_edge, block_edge)

    def fine_slab(packed):
        mixed_here, below_here, above_here, link_ids, live_here, measured = packed
        framed = frame_blocks(mixed_here, below_here, above_here, link_ids, channels)
        predicted = decode(framed, decoder_weight, block_edge, channels)
        residual_here = jnp.where(live_here[:, None, None, None], predicted - measured, 0.0)
        cotangent = (residual_here / CELLS).astype(jnp.bfloat16)
        return (residual_here, cotangent, kernel_term(framed, cotangent, channels))
    residuals, cotangents, decoder_terms = lax.map(fine_slab, (mixed, below_rim.reshape((slab_total,) + plane_shape), above_rim.reshape((slab_total,) + plane_shape), link_all, flat_live, measured_all))
    grad_decoder = lax.optimization_barrier(jnp.sum(decoder_terms, axis=0))
    cot_grid = cotangents.reshape(VOLUMES, SLABS, BLK, block_edge, block_edge, block_edge)
    cot_below, cot_above = neighbour_planes(cot_grid, cot_grid[:, :, :, 0], cot_grid[:, :, :, -1])
    cot_plane = (BLK, block_edge, block_edge)

    def cotangent_slab(packed):
        cot_here, below_here, above_here, link_ids, live_here = packed
        framed_cot = frame_blocks(cot_here, below_here, above_here, link_ids, 1)
        dmixed = spread(framed_cot, decoder_weight, block_edge)
        pooled_cot = pool_sum(dmixed, BLK, half_edge, channels)
        return jnp.where(live_here[:, None, None, None], pooled_cot, 0.0).astype(jnp.bfloat16)
    dupward = lax.map(cotangent_slab, (cotangents, cot_below.reshape((slab_total,) + cot_plane), cot_above.reshape((slab_total,) + cot_plane), link_all, flat_live))
    dcoarse_oct = jnp.zeros((octant_total,) + octant_shape, jnp.bfloat16).at[target_row].set(dupward.reshape((-1,) + octant_shape), mode='drop')
    dcoarse = octants_to_blocks(dcoarse_oct, slab_total * CCAP, half_edge, channels)

    def grad_step(carried, packed):
        block, cot_block, active = packed
        framed = jnp.pad(block[None], ((0, 0), (1, 1), (1, 1), (channels, channels)))
        cot_rows = cot_block.reshape(-1, channels)
        dpre = jnp.where(active, cot_rows, jnp.zeros_like(cot_rows))
        return (carried + coarse_kernel_grad(framed, dpre, block_edge, channels), None)
    grad_rows, unused = lax.scan(grad_step, jnp.zeros((9, 3 * channels, channels), jnp.float32), (coarse_in, dcoarse, coarse_active))
    grad_coarse = grad_rows.reshape(27, channels * channels)
    residual = residuals.reshape(VOLUMES, SLABS, BLK, block_edge, block_edge * block_edge)
    return (residual, grad_coarse, grad_decoder)
```

```python
import jax
import jax.numpy as jnp
from jax import lax
from jax.experimental import pallas as pl
from jax.experimental.pallas import tpu as pltpu
from jax.sharding import PartitionSpec as P

F32 = jnp.float32
BF16 = jnp.bfloat16
VM = pl.BlockSpec(memory_space=pltpu.VMEM)
SM = pl.BlockSpec(memory_space=pltpu.SMEM)
B = 4


def iota(shape, dim):
    return lax.broadcasted_iota(jnp.int32, shape, dim)


def lane_roll(v, shift):
    return pltpu.roll(v, shift % 128, v.ndim - 1)


def group_at(dz, dy):
    if dz == 0:
        return 24 * dy
    if dz == 2:
        return 128 + 24 * dy
    return 72 + 24 * dy if dy < 2 else 128 + 72


def pool_phase(feat_ref, pooled_ref):
    row, col = iota((64, 256), 0), iota((64, 256), 1)
    hit = (row // 8 == col // 32) & (row % 8 == (col % 16) // 2)
    gather = jnp.where(hit, 0.125, 0.0).astype(BF16)
    low = iota((64, 128), 1) < 64
    for b in range(B):
        rows = jnp.dot(gather, feat_ref[b].reshape(256, 1024), preferred_element_type=F32)
        for p in range(4):
            first = rows[:, 256 * p : 256 * p + 128]
            second = rows[:, 256 * p + 128 : 256 * p + 256]
            both = jnp.where(low, first + lane_roll(first, 64), second + lane_roll(second, 64))
            both = both.astype(BF16).astype(F32)
            for z in range(8):
                pooled_ref[z, 8 * b : 8 * b + 8, 128 * p : 128 * p + 128] = both[8 * z : 8 * z + 8]


def coarse_weights(wide_ref, band_ref):
    low = iota((64, 128), 1) < 64
    zero = jnp.zeros((64, 128), F32)
    for k in range(9):
        taps = [wide_ref[3 * k + dx].astype(F32) for dx in range(3)]
        for t in range(2):
            for kx in range(8):
                d0 = kx - 1 - 2 * t
                d1 = d0 - 1
                v0 = taps[d0] if 0 <= d0 < 3 else zero
                v1 = taps[d1] if 0 <= d1 < 3 else zero
                band_ref[k, 64 * kx : 64 * kx + 64, 128 * t : 128 * t + 128] = jnp.where(
                    low, v0, v1
                ).astype(BF16)


def frame_coarse(meta, pooled_ref, sib_ref, frame_ref, zh):
    row = iota((8, 768), 0)

    def masked(cond, v):
        return jnp.where(cond, v, jnp.zeros_like(v))

    def roles(b, col):
        bx, by = meta[b, 0], meta[b, 1]
        found = {}
        for a in range(B):
            ax, ay = meta[a, col], meta[a, col + 1]
            same = (ax >= 0) & (bx >= 0) & ((ax >> 1) == (bx >> 1)) & ((ay >> 1) == (by >> 1))
            for key in ((0, 0), (0, 1), (1, 0), (1, 1)):
                hit = same & ((ax != bx) == bool(key[0])) & ((ay != by) == bool(key[1]))
                found[key] = jnp.where(hit, a, found.get(key, -1))
        return found

    def rows_of(view, who, b):
        xh, yh = meta[b, 0] & 1, meta[b, 1] & 1

        def take(key, lo, hi):
            i = who[key]
            at = pl.multiple_of(jnp.maximum(i, 0) * 8, 8)
            return masked(i >= 0, view(pl.ds(at, 8), slice(lo, hi)))

        def wide(mid, side):
            return jnp.concatenate(
                [
                    masked(xh == 1, take(side, 384, 512)),
                    take(mid, 0, 512),
                    masked(xh == 0, take(side, 0, 128)),
                ],
                axis=1,
            )

        own = wide((0, 0), (1, 0))
        near = wide((0, 1), (1, 1))
        before = jnp.where(row == 0, masked(yh == 1, pltpu.roll(near, 1, 0)), pltpu.roll(own, 1, 0))
        after = jnp.where(row == 7, masked(yh == 0, pltpu.roll(near, 7, 0)), pltpu.roll(own, 7, 0))
        return before, own, after

    own_roles = [roles(b, 0) for b in range(B)]
    sib_roles = [roles(b, 2) for b in range(B)]

    def one_plane(z, unused):
        for q in range(2):
            pair = [
                rows_of(lambda r, c: pooled_ref[z, r, c], own_roles[b], b) for b in (2 * q, 2 * q + 1)
            ]
            for dy in range(3):
                frame_ref[dy, z + 1, 16 * q : 16 * q + 16, :] = jnp.concatenate(
                    [pair[0][dy], pair[1][dy]], axis=0
                ).astype(BF16)
        return unused

    lax.fori_loop(0, 8, one_plane, 0)
    for q in range(2):
        pair = [rows_of(lambda r, c: sib_ref[r, c], sib_roles[b], b) for b in (2 * q, 2 * q + 1)]
        for dy in range(3):
            both = jnp.concatenate([pair[0][dy], pair[1][dy]], axis=0)
            frame_ref[dy, 0, 16 * q : 16 * q + 16, :] = masked(zh == 1, both).astype(BF16)
            frame_ref[dy, 9, 16 * q : 16 * q + 16, :] = masked(zh == 0, both).astype(BF16)


def coarse_conv(frame_ref, band_ref, pre_ref):
    for h in range(2):
        total = None
        for dz in range(3):
            for dy in range(3):
                lhs = frame_ref[dy, dz : dz + 8, :, 256 * h : 256 * h + 512].reshape(256, 512)
                term = jnp.dot(lhs, band_ref[3 * dz + dy], preferred_element_type=F32)
                total = term if total is None else total + term
        pre_ref[:, :, 256 * h : 256 * h + 256] = total.reshape(8, 32, 256)


def mix_phase(meta, feat_ref, pre_ref, up_ref, mixed_ref):
    low = iota((8, 128), 1) < 64

    def one(zc, unused):
        for b in range(B):
            alive = meta[b, 0] >= 0
            for p in range(4):
                v = pre_ref[zc, 8 * b : 8 * b + 8, 128 * p : 128 * p + 128]
                v = jnp.maximum(v, 0.0).astype(BF16).astype(F32)
                turned = lane_roll(v, 64)
                for half in range(2):
                    d = jnp.where(low, v, turned) if half == 0 else jnp.where(low, turned, v)
                    for r in range(2):
                        up_ref[8 * b + 2 * p + half, pl.ds(r, 8, stride=2), :] = d
            for l in range(8):
                u = up_ref[8 * b + l]
                for r in range(2):
                    f = feat_ref[b, 2 * zc + r, :, 128 * l : 128 * l + 128].astype(F32)
                    m = jnp.where(alive, f + u, 0.0)
                    mixed_ref[b, 2 * zc + r, :, 128 * l : 128 * l + 128] = m.astype(BF16)
        return unused

    lax.fori_loop(0, 8, one, 0)


def decoder_bands(wdec_ref, bandt_ref):
    xi = iota((24, 128), 0)
    half = iota((24, 128), 1) // 64
    bandt_ref[...] = jnp.zeros_like(bandt_ref)
    for dz in range(3):
        for dy in range(3):
            taps = [
                jnp.broadcast_to(wdec_ref[9 * dz + 3 * dy + dx : 9 * dz + 3 * dy + dx + 1, :], (24, 128))
                for dx in range(3)
            ]
            at = group_at(dz, dy)
            for l in range(8):
                x = 2 * l + half
                v = jnp.zeros((24, 128), F32)
                for dx in range(3):
                    v = jnp.where(xi == x - dx + 2, taps[dx], v)
                bandt_ref[at : at + 24, 128 * l : 128 * l + 128] = v


def decode_phase(mixed_ref, bandt_ref, tiles_ref, part_ref, up_edge, down_edge):
    lane = iota((16, 128), 1)
    bandt = bandt_ref[...].astype(BF16)
    for b in range(B):
        tiles = lax.dot_general(
            mixed_ref[b].reshape(256, 1024),
            bandt,
            (((1,), (1,)), ((), ())),
            preferred_element_type=F32,
        )
        tiles_ref[...] = tiles.reshape(16, 16, 256)
        up_edge[b] = tiles_ref[15, :, 0:128]
        down_edge[b] = tiles_ref[0, :, 128:256]
        for z in range(16):
            t0, t1 = tiles_ref[z, :, 0:128], tiles_ref[z, :, 128:256]
            v = jnp.where(lane < 48, lane_roll(t0, -72), lane_roll(t1, -24))
            if z > 0:
                v = v + tiles_ref[z - 1, :, 0:128]
            if z < 15:
                v = v + tiles_ref[z + 1, :, 128:256]
            part_ref[b, z] = v


def masked_slot(ref, link):
    v = ref[jnp.maximum(link, 0)]
    return jnp.where(link >= 0, v, jnp.zeros_like(v))


def target_phase(target_ref, wide_ref):
    for y in range(16):
        j, k = y // 8, y % 8
        v = target_ref[:, 128 * j : 128 * j + 128]
        wide_ref[pl.ds(y, 64, stride=16), :] = lane_roll(v, 1 - 16 * k)


def predict_phase(meta, part_ref, below_ref, above_ref, wide_ref, sum_ref, cot_ref, res_ref, out_ref):
    for b in range(B):
        part_ref[b, 0] = part_ref[b, 0] + masked_slot(below_ref, meta[b, 4])
        part_ref[b, 15] = part_ref[b, 15] + masked_slot(above_ref, meta[b, 5])
    row, lane = iota((16, 128), 0), iota((16, 128), 1)
    for b in range(B):
        lo, hi = meta[b, 6], meta[b, 7]

        def along_y(z, unused, b=b, lo=lo, hi=hi):
            own = part_ref[b, z]
            low = part_ref[jnp.maximum(lo, 0), z]
            low = jnp.where(lo >= 0, low, jnp.zeros_like(low))
            high = part_ref[jnp.maximum(hi, 0), z]
            high = jnp.where(hi >= 0, high, jnp.zeros_like(high))
            d0 = jnp.where(row == 0, pltpu.roll(low, 1, 0), pltpu.roll(own, 1, 0))
            d2 = jnp.where(row == 15, pltpu.roll(high, 15, 0), pltpu.roll(own, 15, 0))
            sum_ref[b, z] = d0 + lane_roll(own, -24) + lane_roll(d2, -48)
            return unused

        lax.fori_loop(0, 16, along_y, 0)
    for b in range(B):
        lo, hi = meta[b, 8], meta[b, 9]

        def along_x(z, unused, b=b, lo=lo, hi=hi):
            own = sum_ref[b, z]
            low = sum_ref[jnp.maximum(lo, 0), z]
            high = sum_ref[jnp.maximum(hi, 0), z]
            own = own + jnp.where((lane == 1) & (lo >= 0), lane_roll(low, -16), 0.0)
            own = own + jnp.where((lane == 16) & (hi >= 0), lane_roll(high, 16), 0.0)
            at = pl.multiple_of(256 * b + 16 * z, 16)
            measured = wide_ref[pl.ds(at, 16), :]
            keep = (lane >= 1) & (lane <= 16) & (meta[b, 0] >= 0)
            res = jnp.where(keep, own - measured, 0.0)
            res_ref[pl.ds(at, 16), :] = res
            cot_ref[b, z] = (res * (1.0 / 16384)).astype(BF16).astype(F32)
            return unused

        lax.fori_loop(0, 16, along_x, 0)
    group = iota((64, 128), 1) // 16
    for j in range(2):
        v = jnp.zeros((64, 128), F32)
        for k in range(8):
            got = lane_roll(res_ref[pl.ds(8 * j + k, 64, stride=16), :], 16 * k - 1)
            v = jnp.where(group == k, got, v)
        out_ref[:, 128 * j : 128 * j + 128] = v


def spread_x(lane, own, low, high, lo, hi):
    own = jnp.where(lane == 0, jnp.where(lo >= 0, lane_roll(low, -16), 0.0), own)
    return jnp.where(lane == 17, jnp.where(hi >= 0, lane_roll(high, 16), 0.0), own)


def extend_phase(meta, cot_ref, ext_ref):
    lane = iota((16, 128), 1)
    for b in range(B):
        lo, hi = meta[b, 8], meta[b, 9]

        def along_x(z, unused, b=b, lo=lo, hi=hi):
            low = cot_ref[jnp.maximum(lo, 0), z]
            high = cot_ref[jnp.maximum(hi, 0), z]
            ext_ref[b, z + 1, 8:24, :] = spread_x(lane, cot_ref[b, z], low, high, lo, hi)
            return unused

        lax.fori_loop(0, 16, along_x, 0)
    for b in range(B):
        lo, hi = meta[b, 6], meta[b, 7]
        low = ext_ref[jnp.maximum(lo, 0), 1:17, 23:24, :]
        high = ext_ref[jnp.maximum(hi, 0), 1:17, 8:9, :]
        ext_ref[b, 1:17, 7:8, :] = jnp.where(lo >= 0, low, jnp.zeros_like(low))
        ext_ref[b, 1:17, 24:25, :] = jnp.where(hi >= 0, high, jnp.zeros_like(high))


def adjoint_phase(meta, ext_ref, below_ref, above_ref, taps_ref, cat_ref):
    for b in range(B):
        ext_ref[b, 0] = masked_slot(below_ref, meta[b, 4]).astype(F32)
        ext_ref[b, 17] = masked_slot(above_ref, meta[b, 5]).astype(F32)
    lane = iota((16, 128), 1)
    for b in range(B):

        def gather(z, unused, b=b):
            s0, s1, s2 = (ext_ref[b, z, 9 - dy : 25 - dy, :] for dy in range(3))
            taps_ref[z] = jnp.where(
                lane < 24, s0, jnp.where(lane < 48, lane_roll(s1, 24), lane_roll(s2, 48))
            )
            return unused

        lax.fori_loop(0, 18, gather, 0)

        def place(z, unused, b=b):
            mid = taps_ref[z + 1]
            t0 = jnp.where(lane < 72, taps_ref[z + 2], lane_roll(mid, 72))
            t1 = jnp.where(lane < 72, taps_ref[z], lane_roll(mid, 24))
            cat_ref[b, z] = jnp.concatenate([t0, t1], axis=1).astype(BF16)
            return unused

        lax.fori_loop(0, 16, place, 0)


def decoder_grad(cat_ref, mixed_ref, cross_ref, out_ref):
    cross_ref[...] = lax.dot_general(
        cat_ref[...].reshape(1024, 256),
        mixed_ref[...].reshape(1024, 1024),
        (((0,), (0,)), ((), ())),
        preferred_element_type=F32,
    )
    xi = iota((24, 128), 0)
    half = iota((24, 128), 1) // 64
    for dz in range(3):
        for dy in range(3):
            at = group_at(dz, dy)
            sums = [jnp.zeros((24, 128), F32) for _ in range(3)]
            for l in range(8):
                v = cross_ref[at : at + 24, 128 * l : 128 * l + 128]
                for dx in range(3):
                    sums[dx] = sums[dx] + jnp.where(xi == 2 * l + half - dx + 2, v, 0.0)
            for dx in range(3):
                line = jnp.sum(sums[dx], axis=0, keepdims=True)
                line = line + lane_roll(line, 64)
                tap = 9 * dz + 3 * dy + dx
                out_ref[tap : tap + 1, :] = line


def spread_frame(meta, cot_ref, below_ref, above_ref, tall_ref, full_ref):
    lane = iota((16, 128), 1)
    inner = (lane >= 1) & (lane <= 16)
    for b in range(B):
        for edge, ref, col in ((0, below_ref, 4), (17, above_ref, 5)):
            got = masked_slot(ref, meta[b, col]).astype(F32)[8:24]
            tall_ref[b, edge, 8:24, :] = jnp.where(inner, got, 0.0)
        tall_ref[b, 1:17, 8:24, :] = cot_ref[b]
    for b in range(B):
        lo, hi = meta[b, 6], meta[b, 7]
        low = tall_ref[jnp.maximum(lo, 0), :, 23:24, :]
        high = tall_ref[jnp.maximum(hi, 0), :, 8:9, :]
        tall_ref[b, :, 7:8, :] = jnp.where(lo >= 0, low, jnp.zeros_like(low))
        tall_ref[b, :, 24:25, :] = jnp.where(hi >= 0, high, jnp.zeros_like(high))
    wide = iota((32, 128), 1)
    for b in range(B):
        lo, hi = meta[b, 8], meta[b, 9]

        def along_x(z, unused, b=b, lo=lo, hi=hi):
            low = tall_ref[jnp.maximum(lo, 0), z]
            high = tall_ref[jnp.maximum(hi, 0), z]
            full_ref[b, z] = spread_x(wide, tall_ref[b, z], low, high, lo, hi)
            return unused

        lax.fori_loop(0, 18, along_x, 0)


def spread_gather(full_ref, lhs_ref):
    group = iota((8, 128), 1) // 32

    def planes(z):
        got = []
        for b in range(B):
            v = full_ref[b, z, pl.ds(7, 8, stride=2), :]
            for j in range(1, 4):
                turned = lane_roll(full_ref[b, z, pl.ds(7 + j, 8, stride=2), :], 32 * j)
                v = jnp.where(group == j, turned, v)
            got.append(v)
        return jnp.concatenate(got, axis=0).astype(BF16)

    for z in range(18):
        p = planes(z)
        for i in range(z % 2, 4, 2):
            zc = (z - i) // 2
            if 0 <= zc < 8:
                lhs_ref[zc, :, 128 * i : 128 * i + 128] = p


def spread_weights(wdec_ref, high_ref, low_ref):
    row, col = iota((64, 32), 0), iota((64, 32), 1)

    def pick(k, d):
        return ((k == 2 - d) | (k == 3 - d)).astype(F32)

    sel = pick(row // 16, col // 9) * pick((row // 4) % 4, (col // 3) % 3) * pick(row % 4, col % 3)
    sel = jnp.where(col < 27, sel, 0.0).astype(BF16)
    summed = jnp.dot(sel, wdec_ref[...].astype(BF16), preferred_element_type=F32)
    x = iota((32, 128), 0)
    half = iota((32, 128), 1) // 64
    for ij in range(16):
        taps = [jnp.broadcast_to(summed[4 * ij + k : 4 * ij + k + 1, :], (32, 128)) for k in range(4)]
        for t in range(4):
            v = jnp.zeros((32, 128), F32)
            for k in range(4):
                v = jnp.where(x - 2 * (2 * t + half) == k, taps[k], v)
            hi = v.astype(BF16)
            high_ref[32 * ij : 32 * ij + 32, 128 * t : 128 * t + 128] = hi
            low_ref[32 * ij : 32 * ij + 32, 128 * t : 128 * t + 128] = (v - hi.astype(F32)).astype(BF16)


def dpre_phase(meta, lhs_ref, high_ref, low_ref, pre_ref, dpre_ref):
    lhs = lhs_ref[...].reshape(256, 512)
    up = jnp.dot(lhs, high_ref[...], preferred_element_type=F32)
    up = up + jnp.dot(lhs, low_ref[...], preferred_element_type=F32)
    up = up.astype(BF16).astype(F32).reshape(8, 32, 512)
    for b in range(B):
        mine = up[:, 8 * b : 8 * b + 8]
        keep = (pre_ref[:, 8 * b : 8 * b + 8] > 0) & (meta[b, 0] >= 0)
        dpre_ref[:, 8 * b : 8 * b + 8] = jnp.where(keep, mine, 0.0)


def coarse_grad(frame_ref, dpre_ref, cross_ref, turn_ref, out_ref):
    dpre = dpre_ref[...].reshape(256, 512)
    turned = [dpre[:, 256 * h : 256 * h + 256].T.astype(BF16) for h in range(2)]
    low = iota((64, 128), 1) < 64
    low32 = iota((32, 128), 1) < 64
    pending = []
    for k in range(9):
        dz, dy = k // 3, k % 3
        total = None
        for h in range(2):
            rhs = frame_ref[dy, dz : dz + 8, :, 256 * h : 256 * h + 512].reshape(256, 512)
            term = jnp.dot(turned[h], rhs, preferred_element_type=F32)
            total = term if total is None else total + term
        cross_ref[...] = total
        for dx in range(3):
            sums = [None, None]
            for n in range(4):
                m = n + dx + 1
                v = cross_ref[64 * n : 64 * n + 64, 128 * (m // 2) : 128 * (m // 2) + 128]
                sums[m % 2] = v if sums[m % 2] is None else sums[m % 2] + v
            pending.append((3 * k + dx, sums[0] + lane_roll(sums[1], 64)))
            if len(pending) == 2 or 3 * k + dx == 26:
                first = pending[0][1]
                second = lane_roll(pending[-1][1], 64)
                turn_ref[:, 0:64] = jnp.where(low, first, second).T
                for i, (tap, _) in enumerate(pending):
                    even = turn_ref[pl.ds(64 * i, 32, stride=2), :]
                    odd = turn_ref[pl.ds(64 * i + 1, 32, stride=2), :]
                    out_ref[pl.ds(tap, 32, stride=32), :] = jnp.where(low32, even, lane_roll(odd, 64))
                pending = []


def first_kernel(feat_ref, pooled_ref, plane_ref):
    zh = lax.axis_index("slab") % 2
    pool_phase(feat_ref, pooled_ref)
    plane_ref[...] = pooled_ref[jnp.where(zh == 0, 7, 0)].astype(BF16)


def second_kernel(
    meta, feat_ref, pooled_ref, sib_in, wide_ref, wdec_ref,
    mixed_ref, part_ref, up_edge, down_edge, frame_ref, pre_ref,
    sib_ref, band_ref, up_ref, bandt_ref, tiles_ref,
):
    zh = lax.axis_index("slab") % 2
    coarse_weights(wide_ref, band_ref)
    decoder_bands(wdec_ref, bandt_ref)
    sib_ref[...] = sib_in[...].astype(F32)
    frame_coarse(meta, pooled_ref, sib_ref, frame_ref, zh)
    coarse_conv(frame_ref, band_ref, pre_ref)
    mix_phase(meta, feat_ref, pre_ref, up_ref, mixed_ref)
    decode_phase(mixed_ref, bandt_ref, tiles_ref, part_ref, up_edge, down_edge)


def third_kernel(
    meta, part_in, below_ref, above_ref, target_ref,
    out_ref, cot_ref, low_plane, high_plane, ext_ref,
    part_ref, wide_ref, sum_ref, res_ref,
):
    part_ref[...] = part_in[...]
    target_phase(target_ref, wide_ref)
    predict_phase(meta, part_ref, below_ref, above_ref, wide_ref, sum_ref, cot_ref, res_ref, out_ref)
    extend_phase(meta, cot_ref, ext_ref)
    for b in range(B):
        low_plane[b] = ext_ref[b, 1].astype(BF16)
        high_plane[b] = ext_ref[b, 16].astype(BF16)


def fourth_kernel(
    meta, cot_ref, ext_in, below_ref, above_ref, wdec_ref, mixed_ref, frame_ref, pre_ref,
    dec_ref, coarse_ref,
    ext_ref, taps_ref, cat_ref, dcross_ref, tall_ref, full_ref, lhs_ref, high_ref, low_ref, dpre_ref,
    cross_ref, turn_ref,
):
    ext_ref[...] = ext_in[...]
    adjoint_phase(meta, ext_ref, below_ref, above_ref, taps_ref, cat_ref)
    decoder_grad(cat_ref, mixed_ref, dcross_ref, dec_ref)
    spread_weights(wdec_ref, high_ref, low_ref)
    spread_frame(meta, cot_ref, below_ref, above_ref, tall_ref, full_ref)
    spread_gather(full_ref, lhs_ref)
    dpre_phase(meta, lhs_ref, high_ref, low_ref, pre_ref, dpre_ref)
    coarse_grad(frame_ref, dpre_ref, cross_ref, turn_ref, coarse_ref)


def shape(dims, dtype=F32):
    return jax.ShapeDtypeStruct(dims, dtype)


def call(body, ins, outs, scratch):
    return pl.pallas_call(
        body,
        in_specs=ins,
        out_shape=outs,
        out_specs=[VM] * len(outs),
        scratch_shapes=[pltpu.VMEM(d, t) for d, t in scratch],
        compiler_params=pltpu.CompilerParams(vmem_limit_bytes=48 * 1024 * 1024),
    )


def per_device(features, target, block_coords, neighbours, owners, coarse_weight, decoder_weight):
    feat = features[0, 0]
    coords = block_coords[0, 0]
    count = lax.axis_size("slab")
    sib_coords = lax.ppermute(coords, "slab", [(i, i ^ 1) for i in range(count)])
    meta = jnp.concatenate(
        [coords, sib_coords, neighbours[0, 0], jnp.zeros((B, 6), jnp.int32)], axis=1
    )
    w3 = coarse_weight.reshape(27, 64, 64)
    wide = jnp.concatenate([w3, w3], axis=2)
    wdec = jnp.pad(
        jnp.concatenate([decoder_weight, decoder_weight], axis=1).astype(F32), ((0, 5), (0, 0))
    )
    pooled, plane = call(
        first_kernel, [VM], [shape((8, 32, 512)), shape((32, 512), BF16)], []
    )(feat)
    sib = lax.ppermute(plane, "slab", [(i, i ^ 1) for i in range(count)])
    mixed, part, up_edge, down_edge, frame, pre = call(
        second_kernel,
        [SM] + [VM] * 5,
        [
            shape((4, 16, 16, 1024), BF16),
            shape((4, 16, 16, 128)),
            shape((4, 16, 128)),
            shape((4, 16, 128)),
            shape((3, 10, 32, 768), BF16),
            shape((8, 32, 512)),
        ],
        [
            ((32, 512), F32),
            ((9, 512, 256), BF16),
            ((32, 16, 128), F32),
            ((256, 1024), F32),
            ((16, 16, 256), F32),
        ],
    )(meta, feat, pooled, sib, wide, wdec)
    up = [(i, i + 1) for i in range(count - 1)]
    down = [(j, i) for i, j in up]
    below = lax.ppermute(up_edge, "slab", up)
    above = lax.ppermute(down_edge, "slab", down)
    res, cot, low_plane, high_plane, ext = call(
        third_kernel,
        [SM] + [VM] * 4,
        [
            shape((64, 256)),
            shape((4, 16, 16, 128)),
            shape((4, 32, 128), BF16),
            shape((4, 32, 128), BF16),
            shape((4, 18, 32, 128)),
        ],
        [
            ((4, 16, 16, 128), F32),
            ((1024, 128), F32),
            ((4, 16, 16, 128), F32),
            ((1024, 128), F32),
        ],
    )(meta, part, below, above, target[0, 0].reshape(64, 256))
    cot_below = lax.ppermute(high_plane, "slab", up)
    cot_above = lax.ppermute(low_plane, "slab", down)
    dec, coarse = call(
        fourth_kernel,
        [SM] + [VM] * 8,
        [shape((32, 128)), shape((1024, 128))],
        [
            ((4, 18, 32, 128), F32),
            ((18, 16, 128), F32),
            ((4, 16, 16, 256), BF16),
            ((256, 1024), F32),
            ((4, 18, 32, 128), F32),
            ((4, 18, 32, 128), F32),
            ((8, 32, 512), BF16),
            ((512, 512), BF16),
            ((512, 512), BF16),
            ((8, 32, 512), F32),
            ((256, 512), F32),
            ((128, 128), F32),
        ],
    )(meta, cot, ext, cot_below, cot_above, wdec, mixed, frame, pre)
    mine = lax.psum_scatter(coarse.reshape(32, 32, 128), "slab", scatter_dimension=0, tiled=False)
    mine = lax.psum(mine, "dp")[:27]
    dec = lax.psum(dec[:27, :64], ("dp", "slab"))
    return res.reshape(1, 1, B, 16, 256), mine, dec


def solution(mesh):
    placed = (
        P("dp", "slab", None, None, None, None),
        P("dp", "slab", None, None, None),
        P("dp", "slab", None, None),
        P("dp", "slab", None, None),
        P("dp", "slab", None, None),
        P(),
        P(),
    )
    return jax.shard_map(
        per_device,
        mesh=mesh,
        in_specs=placed,
        out_specs=(P("dp", "slab", None, None, None), P(None, "slab"), P()),
        check_vma=False,
    )
```

```python
import jax
import jax.numpy as jnp
from jax import lax
from jax.experimental import pallas as pl
from jax.experimental.pallas import tpu as pltpu
from jax.sharding import PartitionSpec as P

F32 = jnp.float32
BF16 = jnp.bfloat16
VM = pl.BlockSpec(memory_space=pltpu.VMEM)
SM = pl.BlockSpec(memory_space=pltpu.SMEM)
B = 4


def iota(shape, dim):
    return lax.broadcasted_iota(jnp.int32, shape, dim)


def repeat(count, body, step):
    def some(i, unused):
        for k in range(step):
            body(i * step + k)
        return unused

    if step == count:
        some(0, 0)
    else:
        lax.fori_loop(0, count // step, some, 0)


def lane_roll(v, shift):
    return pltpu.roll(v, shift % 128, v.ndim - 1)


def group_at(dz, dy):
    if dz == 0:
        return 24 * dy
    if dz == 2:
        return 128 + 24 * dy
    return 72 + 24 * dy if dy < 2 else 128 + 72


def pool_phase(feat_ref, pooled_ref):
    row, col = iota((64, 256), 0), iota((64, 256), 1)
    hit = (row // 8 == col // 32) & (row % 8 == (col % 16) // 2)
    gather = jnp.where(hit, 0.125, 0.0).astype(BF16)
    low = iota((64, 128), 1) < 64
    for b in range(B):
        rows = jnp.dot(gather, feat_ref[b].reshape(256, 1024), preferred_element_type=F32)
        for p in range(4):
            first = rows[:, 256 * p : 256 * p + 128]
            second = rows[:, 256 * p + 128 : 256 * p + 256]
            both = jnp.where(low, first + lane_roll(first, 64), second + lane_roll(second, 64))
            both = both.astype(BF16).astype(F32)
            for z in range(8):
                pooled_ref[z, 8 * b : 8 * b + 8, 128 * p : 128 * p + 128] = both[8 * z : 8 * z + 8]


def coarse_weights(wide_ref, band_ref):
    low = iota((64, 128), 1) < 64
    zero = jnp.zeros((64, 128), F32)
    for k in range(9):
        taps = [wide_ref[3 * k + dx].astype(F32) for dx in range(3)]
        for t in range(2):
            for kx in range(8):
                d0 = kx - 1 - 2 * t
                d1 = d0 - 1
                v0 = taps[d0] if 0 <= d0 < 3 else zero
                v1 = taps[d1] if 0 <= d1 < 3 else zero
                band_ref[k, 64 * kx : 64 * kx + 64, 128 * t : 128 * t + 128] = jnp.where(
                    low, v0, v1
                ).astype(BF16)


def frame_coarse(meta, pooled_ref, sib_ref, frame_ref, zh):
    row = iota((8, 768), 0)

    def masked(cond, v):
        return jnp.where(cond, v, jnp.zeros_like(v))

    def roles(b, col):
        bx, by = meta[b, 0], meta[b, 1]
        found = {}
        for a in range(B):
            ax, ay = meta[a, col], meta[a, col + 1]
            same = (ax >= 0) & (bx >= 0) & ((ax >> 1) == (bx >> 1)) & ((ay >> 1) == (by >> 1))
            for key in ((0, 0), (0, 1), (1, 0), (1, 1)):
                hit = same & ((ax != bx) == bool(key[0])) & ((ay != by) == bool(key[1]))
                found[key] = jnp.where(hit, a, found.get(key, -1))
        return found

    def rows_of(view, who, b):
        xh, yh = meta[b, 0] & 1, meta[b, 1] & 1

        def take(key, lo, hi):
            i = who[key]
            at = pl.multiple_of(jnp.maximum(i, 0) * 8, 8)
            return masked(i >= 0, view(pl.ds(at, 8), slice(lo, hi)))

        def wide(mid, side):
            return jnp.concatenate(
                [
                    masked(xh == 1, take(side, 384, 512)),
                    take(mid, 0, 512),
                    masked(xh == 0, take(side, 0, 128)),
                ],
                axis=1,
            )

        own = wide((0, 0), (1, 0))
        near = wide((0, 1), (1, 1))
        before = jnp.where(row == 0, masked(yh == 1, pltpu.roll(near, 1, 0)), pltpu.roll(own, 1, 0))
        after = jnp.where(row == 7, masked(yh == 0, pltpu.roll(near, 7, 0)), pltpu.roll(own, 7, 0))
        return before, own, after

    own_roles = [roles(b, 0) for b in range(B)]
    sib_roles = [roles(b, 2) for b in range(B)]

    def one_plane(z):
        for q in range(2):
            pair = [
                rows_of(lambda r, c: pooled_ref[z, r, c], own_roles[b], b) for b in (2 * q, 2 * q + 1)
            ]
            for dy in range(3):
                frame_ref[dy, z + 1, 16 * q : 16 * q + 16, :] = jnp.concatenate(
                    [pair[0][dy], pair[1][dy]], axis=0
                ).astype(BF16)

    repeat(8, one_plane, 2)
    for q in range(2):
        pair = [rows_of(lambda r, c: sib_ref[r, c], sib_roles[b], b) for b in (2 * q, 2 * q + 1)]
        for dy in range(3):
            both = jnp.concatenate([pair[0][dy], pair[1][dy]], axis=0)
            frame_ref[dy, 0, 16 * q : 16 * q + 16, :] = masked(zh == 1, both).astype(BF16)
            frame_ref[dy, 9, 16 * q : 16 * q + 16, :] = masked(zh == 0, both).astype(BF16)


def coarse_conv(frame_ref, band_ref, pre_ref):
    for h in range(2):
        total = None
        for dz in range(3):
            for dy in range(3):
                lhs = frame_ref[dy, dz : dz + 8, :, 256 * h : 256 * h + 512].reshape(256, 512)
                term = jnp.dot(lhs, band_ref[3 * dz + dy], preferred_element_type=F32)
                total = term if total is None else total + term
        pre_ref[:, :, 256 * h : 256 * h + 256] = total.reshape(8, 32, 256)


def mix_phase(meta, feat_ref, pre_ref, up_ref, mixed_ref):
    low = iota((8, 128), 1) < 64

    def one(zc):
        for b in range(B):
            alive = meta[b, 0] >= 0
            for p in range(4):
                v = pre_ref[zc, 8 * b : 8 * b + 8, 128 * p : 128 * p + 128]
                v = jnp.maximum(v, 0.0).astype(BF16).astype(F32)
                turned = lane_roll(v, 64)
                for half in range(2):
                    d = jnp.where(low, v, turned) if half == 0 else jnp.where(low, turned, v)
                    for r in range(2):
                        up_ref[8 * b + 2 * p + half, pl.ds(r, 8, stride=2), :] = d
            for l in range(8):
                u = up_ref[8 * b + l]
                for r in range(2):
                    f = feat_ref[b, 2 * zc + r, :, 128 * l : 128 * l + 128].astype(F32)
                    m = jnp.where(alive, f + u, 0.0)
                    mixed_ref[b, 2 * zc + r, :, 128 * l : 128 * l + 128] = m.astype(BF16)

    repeat(8, one, 1)


def decoder_bands(wdec_ref, bandt_ref):
    xi = iota((24, 128), 0)
    half = iota((24, 128), 1) // 64
    bandt_ref[...] = jnp.zeros_like(bandt_ref)
    for dz in range(3):
        for dy in range(3):
            taps = [
                jnp.broadcast_to(wdec_ref[9 * dz + 3 * dy + dx : 9 * dz + 3 * dy + dx + 1, :], (24, 128))
                for dx in range(3)
            ]
            at = group_at(dz, dy)
            for l in range(8):
                x = 2 * l + half
                v = jnp.zeros((24, 128), F32)
                for dx in range(3):
                    v = jnp.where(xi == x - dx + 2, taps[dx], v)
                bandt_ref[at : at + 24, 128 * l : 128 * l + 128] = v


def decode_phase(mixed_ref, bandt_ref, tiles_ref, part_ref, up_edge, down_edge):
    lane = iota((16, 128), 1)
    bandt = bandt_ref[...].astype(BF16)
    for b in range(B):
        tiles = lax.dot_general(
            mixed_ref[b].reshape(256, 1024),
            bandt,
            (((1,), (1,)), ((), ())),
            preferred_element_type=F32,
        )
        tiles_ref[...] = tiles.reshape(16, 16, 256)
        up_edge[b] = tiles_ref[15, :, 0:128]
        down_edge[b] = tiles_ref[0, :, 128:256]
        for z in range(16):
            t0, t1 = tiles_ref[z, :, 0:128], tiles_ref[z, :, 128:256]
            v = jnp.where(lane < 48, lane_roll(t0, -72), lane_roll(t1, -24))
            if z > 0:
                v = v + tiles_ref[z - 1, :, 0:128]
            if z < 15:
                v = v + tiles_ref[z + 1, :, 128:256]
            part_ref[b, z] = v


def masked_slot(ref, link):
    v = ref[jnp.maximum(link, 0)]
    return jnp.where(link >= 0, v, jnp.zeros_like(v))


def target_phase(target_ref, wide_ref):
    for y in range(16):
        j, k = y // 8, y % 8
        v = target_ref[:, 128 * j : 128 * j + 128]
        wide_ref[pl.ds(y, 64, stride=16), :] = lane_roll(v, 1 - 16 * k)


def predict_phase(meta, part_ref, below_ref, above_ref, wide_ref, sum_ref, cot_ref, res_ref, out_ref):
    for b in range(B):
        part_ref[b, 0] = part_ref[b, 0] + masked_slot(below_ref, meta[b, 4])
        part_ref[b, 15] = part_ref[b, 15] + masked_slot(above_ref, meta[b, 5])
    row, lane = iota((16, 128), 0), iota((16, 128), 1)
    for b in range(B):
        lo, hi = meta[b, 6], meta[b, 7]

        def along_y(z, b=b, lo=lo, hi=hi):
            own = part_ref[b, z]
            low = part_ref[jnp.maximum(lo, 0), z]
            low = jnp.where(lo >= 0, low, jnp.zeros_like(low))
            high = part_ref[jnp.maximum(hi, 0), z]
            high = jnp.where(hi >= 0, high, jnp.zeros_like(high))
            d0 = jnp.where(row == 0, pltpu.roll(low, 1, 0), pltpu.roll(own, 1, 0))
            d2 = jnp.where(row == 15, pltpu.roll(high, 15, 0), pltpu.roll(own, 15, 0))
            sum_ref[b, z] = d0 + lane_roll(own, -24) + lane_roll(d2, -48)

        repeat(16, along_y, 8)
    for b in range(B):
        lo, hi = meta[b, 8], meta[b, 9]

        def along_x(z, b=b, lo=lo, hi=hi):
            own = sum_ref[b, z]
            low = sum_ref[jnp.maximum(lo, 0), z]
            high = sum_ref[jnp.maximum(hi, 0), z]
            own = own + jnp.where((lane == 1) & (lo >= 0), lane_roll(low, -16), 0.0)
            own = own + jnp.where((lane == 16) & (hi >= 0), lane_roll(high, 16), 0.0)
            at = pl.multiple_of(256 * b + 16 * z, 16)
            measured = wide_ref[pl.ds(at, 16), :]
            keep = (lane >= 1) & (lane <= 16) & (meta[b, 0] >= 0)
            res = jnp.where(keep, own - measured, 0.0)
            res_ref[pl.ds(at, 16), :] = res
            cot_ref[b, z] = (res * (1.0 / 16384)).astype(BF16).astype(F32)

        repeat(16, along_x, 8)
    group = iota((64, 128), 1) // 16
    for j in range(2):
        v = jnp.zeros((64, 128), F32)
        for k in range(8):
            got = lane_roll(res_ref[pl.ds(8 * j + k, 64, stride=16), :], 16 * k - 1)
            v = jnp.where(group == k, got, v)
        out_ref[:, 128 * j : 128 * j + 128] = v


def spread_x(lane, own, low, high, lo, hi):
    own = jnp.where(lane == 0, jnp.where(lo >= 0, lane_roll(low, -16), 0.0), own)
    return jnp.where(lane == 17, jnp.where(hi >= 0, lane_roll(high, 16), 0.0), own)


def extend_phase(meta, cot_ref, ext_ref):
    lane = iota((16, 128), 1)
    for b in range(B):
        lo, hi = meta[b, 8], meta[b, 9]

        def along_x(z, b=b, lo=lo, hi=hi):
            low = cot_ref[jnp.maximum(lo, 0), z]
            high = cot_ref[jnp.maximum(hi, 0), z]
            ext_ref[b, z + 1, 8:24, :] = spread_x(lane, cot_ref[b, z], low, high, lo, hi)

        repeat(16, along_x, 8)
    for b in range(B):
        lo, hi = meta[b, 6], meta[b, 7]
        low = ext_ref[jnp.maximum(lo, 0), 1:17, 23:24, :]
        high = ext_ref[jnp.maximum(hi, 0), 1:17, 8:9, :]
        ext_ref[b, 1:17, 7:8, :] = jnp.where(lo >= 0, low, jnp.zeros_like(low))
        ext_ref[b, 1:17, 24:25, :] = jnp.where(hi >= 0, high, jnp.zeros_like(high))


def adjoint_phase(meta, ext_ref, below_ref, above_ref, taps_ref, cat_ref):
    for b in range(B):
        ext_ref[b, 0] = masked_slot(below_ref, meta[b, 4]).astype(F32)
        ext_ref[b, 17] = masked_slot(above_ref, meta[b, 5]).astype(F32)
    lane = iota((16, 128), 1)
    for b in range(B):

        def gather(z, b=b):
            s0, s1, s2 = (ext_ref[b, z, 9 - dy : 25 - dy, :] for dy in range(3))
            taps_ref[z] = jnp.where(
                lane < 24, s0, jnp.where(lane < 48, lane_roll(s1, 24), lane_roll(s2, 48))
            )

        repeat(18, gather, 9)

        def place(z, b=b):
            mid = taps_ref[z + 1]
            t0 = jnp.where(lane < 72, taps_ref[z + 2], lane_roll(mid, 72))
            t1 = jnp.where(lane < 72, taps_ref[z], lane_roll(mid, 24))
            cat_ref[b, z] = jnp.concatenate([t0, t1], axis=1).astype(BF16)

        repeat(16, place, 8)


def decoder_grad(cat_ref, mixed_ref, cross_ref, out_ref):
    cross_ref[...] = lax.dot_general(
        cat_ref[...].reshape(1024, 256),
        mixed_ref[...].reshape(1024, 1024),
        (((0,), (0,)), ((), ())),
        preferred_element_type=F32,
    )
    xi = iota((24, 128), 0)
    half = iota((24, 128), 1) // 64
    for dz in range(3):
        for dy in range(3):
            at = group_at(dz, dy)
            sums = [jnp.zeros((24, 128), F32) for _ in range(3)]
            for l in range(8):
                v = cross_ref[at : at + 24, 128 * l : 128 * l + 128]
                for dx in range(3):
                    sums[dx] = sums[dx] + jnp.where(xi == 2 * l + half - dx + 2, v, 0.0)
            for dx in range(3):
                line = jnp.sum(sums[dx], axis=0, keepdims=True)
                line = line + lane_roll(line, 64)
                tap = 9 * dz + 3 * dy + dx
                out_ref[tap : tap + 1, :] = line


def spread_frame(meta, cot_ref, below_ref, above_ref, tall_ref, full_ref):
    lane = iota((16, 128), 1)
    inner = (lane >= 1) & (lane <= 16)
    for b in range(B):
        for edge, ref, col in ((0, below_ref, 4), (17, above_ref, 5)):
            got = masked_slot(ref, meta[b, col]).astype(F32)[8:24]
            tall_ref[b, edge, 8:24, :] = jnp.where(inner, got, 0.0)
        tall_ref[b, 1:17, 8:24, :] = cot_ref[b]
    for b in range(B):
        lo, hi = meta[b, 6], meta[b, 7]
        low = tall_ref[jnp.maximum(lo, 0), :, 23:24, :]
        high = tall_ref[jnp.maximum(hi, 0), :, 8:9, :]
        tall_ref[b, :, 7:8, :] = jnp.where(lo >= 0, low, jnp.zeros_like(low))
        tall_ref[b, :, 24:25, :] = jnp.where(hi >= 0, high, jnp.zeros_like(high))
    wide = iota((32, 128), 1)
    for b in range(B):
        lo, hi = meta[b, 8], meta[b, 9]

        def along_x(z, b=b, lo=lo, hi=hi):
            low = tall_ref[jnp.maximum(lo, 0), z]
            high = tall_ref[jnp.maximum(hi, 0), z]
            full_ref[b, z] = spread_x(wide, tall_ref[b, z], low, high, lo, hi)

        repeat(18, along_x, 9)


def spread_gather(full_ref, lhs_ref):
    group = iota((8, 128), 1) // 32

    def planes(z):
        got = []
        for b in range(B):
            v = full_ref[b, z, pl.ds(7, 8, stride=2), :]
            for j in range(1, 4):
                turned = lane_roll(full_ref[b, z, pl.ds(7 + j, 8, stride=2), :], 32 * j)
                v = jnp.where(group == j, turned, v)
            got.append(v)
        return jnp.concatenate(got, axis=0).astype(BF16)

    for z in range(18):
        p = planes(z)
        for i in range(z % 2, 4, 2):
            zc = (z - i) // 2
            if 0 <= zc < 8:
                lhs_ref[zc, :, 128 * i : 128 * i + 128] = p


def spread_weights(wdec_ref, high_ref, low_ref):
    row, col = iota((64, 32), 0), iota((64, 32), 1)

    def pick(k, d):
        return ((k == 2 - d) | (k == 3 - d)).astype(F32)

    sel = pick(row // 16, col // 9) * pick((row // 4) % 4, (col // 3) % 3) * pick(row % 4, col % 3)
    sel = jnp.where(col < 27, sel, 0.0).astype(BF16)
    summed = jnp.dot(sel, wdec_ref[...].astype(BF16), preferred_element_type=F32)
    x = iota((32, 128), 0)
    half = iota((32, 128), 1) // 64
    for ij in range(16):
        taps = [jnp.broadcast_to(summed[4 * ij + k : 4 * ij + k + 1, :], (32, 128)) for k in range(4)]
        for t in range(4):
            v = jnp.zeros((32, 128), F32)
            for k in range(4):
                v = jnp.where(x - 2 * (2 * t + half) == k, taps[k], v)
            hi = v.astype(BF16)
            high_ref[32 * ij : 32 * ij + 32, 128 * t : 128 * t + 128] = hi
            low_ref[32 * ij : 32 * ij + 32, 128 * t : 128 * t + 128] = (v - hi.astype(F32)).astype(BF16)


def dpre_phase(meta, lhs_ref, high_ref, low_ref, pre_ref, dpre_ref):
    lhs = lhs_ref[...].reshape(256, 512)
    up = jnp.dot(lhs, high_ref[...], preferred_element_type=F32)
    up = up + jnp.dot(lhs, low_ref[...], preferred_element_type=F32)
    up = up.astype(BF16).astype(F32).reshape(8, 32, 512)
    for b in range(B):
        mine = up[:, 8 * b : 8 * b + 8]
        keep = (pre_ref[:, 8 * b : 8 * b + 8] > 0) & (meta[b, 0] >= 0)
        dpre_ref[:, 8 * b : 8 * b + 8] = jnp.where(keep, mine, 0.0)


def coarse_grad(frame_ref, dpre_ref, cross_ref, turn_ref, out_ref):
    dpre = dpre_ref[...].reshape(256, 512)
    turned = [dpre[:, 256 * h : 256 * h + 256].T.astype(BF16) for h in range(2)]
    low = iota((64, 128), 1) < 64
    low32 = iota((32, 128), 1) < 64
    pending = []
    for k in range(9):
        dz, dy = k // 3, k % 3
        total = None
        for h in range(2):
            rhs = frame_ref[dy, dz : dz + 8, :, 256 * h : 256 * h + 512].reshape(256, 512)
            term = jnp.dot(turned[h], rhs, preferred_element_type=F32)
            total = term if total is None else total + term
        cross_ref[...] = total
        for dx in range(3):
            sums = [None, None]
            for n in range(4):
                m = n + dx + 1
                v = cross_ref[64 * n : 64 * n + 64, 128 * (m // 2) : 128 * (m // 2) + 128]
                sums[m % 2] = v if sums[m % 2] is None else sums[m % 2] + v
            pending.append((3 * k + dx, sums[0] + lane_roll(sums[1], 64)))
            if len(pending) == 2 or 3 * k + dx == 26:
                first = pending[0][1]
                second = lane_roll(pending[-1][1], 64)
                turn_ref[:, 0:64] = jnp.where(low, first, second).T
                for i, (tap, _) in enumerate(pending):
                    even = turn_ref[pl.ds(64 * i, 32, stride=2), :]
                    odd = turn_ref[pl.ds(64 * i + 1, 32, stride=2), :]
                    out_ref[pl.ds(tap, 32, stride=48), :] = jnp.where(low32, even, lane_roll(odd, 64))
                pending = []


def first_kernel(feat_ref, pooled_ref, plane_ref):
    zh = lax.axis_index("slab") % 2
    pool_phase(feat_ref, pooled_ref)
    plane_ref[...] = pooled_ref[jnp.where(zh == 0, 7, 0)].astype(BF16)


def second_kernel(
    meta, feat_ref, pooled_ref, sib_in, wide_ref, wdec_ref,
    mixed_ref, part_ref, up_edge, down_edge, frame_ref, pre_ref,
    sib_ref, band_ref, up_ref, bandt_ref, tiles_ref,
):
    zh = lax.axis_index("slab") % 2
    coarse_weights(wide_ref, band_ref)
    decoder_bands(wdec_ref, bandt_ref)
    sib_ref[...] = sib_in[...].astype(F32)
    frame_coarse(meta, pooled_ref, sib_ref, frame_ref, zh)
    coarse_conv(frame_ref, band_ref, pre_ref)
    mix_phase(meta, feat_ref, pre_ref, up_ref, mixed_ref)
    decode_phase(mixed_ref, bandt_ref, tiles_ref, part_ref, up_edge, down_edge)


def third_kernel(
    meta, part_in, below_ref, above_ref, target_ref,
    out_ref, cot_ref, low_plane, high_plane, ext_ref,
    part_ref, wide_ref, sum_ref, res_ref,
):
    part_ref[...] = part_in[...]
    target_phase(target_ref, wide_ref)
    predict_phase(meta, part_ref, below_ref, above_ref, wide_ref, sum_ref, cot_ref, res_ref, out_ref)
    extend_phase(meta, cot_ref, ext_ref)
    for b in range(B):
        low_plane[b] = ext_ref[b, 1].astype(BF16)
        high_plane[b] = ext_ref[b, 16].astype(BF16)


def fourth_kernel(
    meta, cot_ref, ext_in, below_ref, above_ref, wdec_ref, mixed_ref, frame_ref, pre_ref,
    coarse_ref,
    dec_ref, ext_ref, taps_ref, cat_ref, dcross_ref, tall_ref, full_ref, lhs_ref, high_ref, low_ref, dpre_ref,
    cross_ref, turn_ref,
):
    ext_ref[...] = ext_in[...]
    adjoint_phase(meta, ext_ref, below_ref, above_ref, taps_ref, cat_ref)
    decoder_grad(cat_ref, mixed_ref, dcross_ref, dec_ref)
    even = dec_ref[pl.ds(0, 16, stride=2), :]
    odd = dec_ref[pl.ds(1, 16, stride=2), :]
    both = jnp.where(iota((16, 128), 1) < 64, even, odd)
    for j in range(32):
        coarse_ref[48 * j + 32 : 48 * j + 48, :] = both
    spread_weights(wdec_ref, high_ref, low_ref)
    spread_frame(meta, cot_ref, below_ref, above_ref, tall_ref, full_ref)
    spread_gather(full_ref, lhs_ref)
    dpre_phase(meta, lhs_ref, high_ref, low_ref, pre_ref, dpre_ref)
    coarse_grad(frame_ref, dpre_ref, cross_ref, turn_ref, coarse_ref)


def reduce_kernel(
    local_ref, coarse_ref, dec_ref,
    sib_ref, half_ref, chips_ref, parts_ref, pair_sems, chip_sends, chip_recvs, dp_sends, dp_recvs,
):
    slab, dp = lax.axis_index("slab"), lax.axis_index("dp")
    core, chip = slab % 2, slab // 2
    chips, copies = chips_ref.shape[0], parts_ref.shape[0]
    sibling = {"slab": slab + 1 - 2 * core}
    barrier = pltpu.get_barrier_semaphore()

    def greet(device):
        pl.semaphore_signal(barrier, inc=1, device_id=device, device_id_type=pl.DeviceIdType.MESH)

    def peer(r):
        return lax.rem(chip + r, chips)

    def twin(r):
        return lax.rem(dp + r, copies)

    greet(sibling)
    for r in range(1, chips):
        greet({"slab": 2 * peer(r) + core})
    for r in range(1, copies):
        greet({"dp": twin(r)})
    pl.semaphore_wait(barrier, chips + copies - 1)

    swap = pltpu.make_async_remote_copy(
        src_ref=local_ref.at[:, 1 - core],
        dst_ref=sib_ref,
        send_sem=pair_sems.at[0],
        recv_sem=pair_sems.at[1],
        device_id=sibling,
        device_id_type=pl.DeviceIdType.MESH,
    )
    swap.start()
    swap.wait()
    half_ref[...] = local_ref[:, core] + sib_ref[...]

    def to_chip(r):
        return pltpu.make_async_remote_copy(
            src_ref=half_ref.at[peer(r)],
            dst_ref=chips_ref.at[chip],
            send_sem=chip_sends.at[r],
            recv_sem=chip_recvs.at[chip],
            device_id={"slab": 2 * peer(r) + core},
            device_id_type=pl.DeviceIdType.MESH,
        )

    def from_chip(r):
        return pltpu.make_async_remote_copy(
            src_ref=half_ref.at[chip],
            dst_ref=chips_ref.at[peer(r)],
            send_sem=chip_sends.at[r],
            recv_sem=chip_recvs.at[peer(r)],
            device_id={"slab": 2 * peer(r) + core},
            device_id_type=pl.DeviceIdType.MESH,
        )

    for r in range(1, chips):
        to_chip(r).start()
    chips_ref[chip] = half_ref[chip]
    for r in range(1, chips):
        from_chip(r).wait_recv()
    total = chips_ref[0]
    for k in range(1, chips):
        total = total + chips_ref[k]
    parts_ref[dp] = total

    def to_twin(r):
        return pltpu.make_async_remote_copy(
            src_ref=parts_ref.at[dp],
            dst_ref=parts_ref.at[dp],
            send_sem=dp_sends.at[r],
            recv_sem=dp_recvs.at[dp],
            device_id={"dp": twin(r)},
            device_id_type=pl.DeviceIdType.MESH,
        )

    def from_twin(r):
        return pltpu.make_async_remote_copy(
            src_ref=parts_ref.at[dp],
            dst_ref=parts_ref.at[twin(r)],
            send_sem=dp_sends.at[r],
            recv_sem=dp_recvs.at[twin(r)],
            device_id={"dp": twin(r)},
            device_id_type=pl.DeviceIdType.MESH,
        )

    for r in range(1, copies):
        to_twin(r).start()
    for r in range(1, copies):
        from_twin(r).wait_recv()
    total = parts_ref[0]
    for k in range(1, copies):
        total = total + parts_ref[k]
    coarse_ref[...] = total[0:27]
    for tap in range(27):
        line = total[32 + tap // 2 : 33 + tap // 2]
        dec_ref[tap : tap + 1, :] = line[:, 64 * (tap % 2) : 64 * (tap % 2) + 64]
    for r in range(1, chips):
        to_chip(r).wait_send()
    for r in range(1, copies):
        to_twin(r).wait_send()


def shape(dims, dtype=F32):
    return jax.ShapeDtypeStruct(dims, dtype)


def call(body, ins, outs, scratch):
    return pl.pallas_call(
        body,
        in_specs=ins,
        out_shape=outs,
        out_specs=[VM] * len(outs),
        scratch_shapes=[pltpu.VMEM(d, t) for d, t in scratch],
        compiler_params=pltpu.CompilerParams(vmem_limit_bytes=48 * 1024 * 1024),
    )


def per_device(features, target, block_coords, neighbours, owners, coarse_weight, decoder_weight):
    feat = features[0, 0]
    coords = block_coords[0, 0]
    count = lax.axis_size("slab")
    sib_coords = lax.ppermute(coords, "slab", [(i, i ^ 1) for i in range(count)])
    meta = jnp.concatenate(
        [coords, sib_coords, neighbours[0, 0], jnp.zeros((B, 6), jnp.int32)], axis=1
    )
    w3 = coarse_weight.reshape(27, 64, 64)
    wide = jnp.concatenate([w3, w3], axis=2)
    wdec = jnp.pad(
        jnp.concatenate([decoder_weight, decoder_weight], axis=1).astype(F32), ((0, 5), (0, 0))
    )
    pooled, plane = call(
        first_kernel, [VM], [shape((8, 32, 512)), shape((32, 512), BF16)], []
    )(feat)
    sib = lax.ppermute(plane, "slab", [(i, i ^ 1) for i in range(count)])
    mixed, part, up_edge, down_edge, frame, pre = call(
        second_kernel,
        [SM] + [VM] * 5,
        [
            shape((4, 16, 16, 1024), BF16),
            shape((4, 16, 16, 128)),
            shape((4, 16, 128)),
            shape((4, 16, 128)),
            shape((3, 10, 32, 768), BF16),
            shape((8, 32, 512)),
        ],
        [
            ((32, 512), F32),
            ((9, 512, 256), BF16),
            ((32, 16, 128), F32),
            ((256, 1024), F32),
            ((16, 16, 256), F32),
        ],
    )(meta, feat, pooled, sib, wide, wdec)
    up = [(i, i + 1) for i in range(count - 1)]
    down = [(j, i) for i, j in up]
    below = lax.ppermute(up_edge, "slab", up)
    above = lax.ppermute(down_edge, "slab", down)
    res, cot, low_plane, high_plane, ext = call(
        third_kernel,
        [SM] + [VM] * 4,
        [
            shape((64, 256)),
            shape((4, 16, 16, 128)),
            shape((4, 32, 128), BF16),
            shape((4, 32, 128), BF16),
            shape((4, 18, 32, 128)),
        ],
        [
            ((4, 16, 16, 128), F32),
            ((1024, 128), F32),
            ((4, 16, 16, 128), F32),
            ((1024, 128), F32),
        ],
    )(meta, part, below, above, target[0, 0].reshape(64, 256))
    cot_below = lax.ppermute(high_plane, "slab", up)
    cot_above = lax.ppermute(low_plane, "slab", down)
    (coarse,) = call(
        fourth_kernel,
        [SM] + [VM] * 8,
        [shape((1536, 128))],
        [
            ((32, 128), F32),
            ((4, 18, 32, 128), F32),
            ((18, 16, 128), F32),
            ((4, 16, 16, 256), BF16),
            ((256, 1024), F32),
            ((4, 18, 32, 128), F32),
            ((4, 18, 32, 128), F32),
            ((8, 32, 512), BF16),
            ((512, 512), BF16),
            ((512, 512), BF16),
            ((8, 32, 512), F32),
            ((256, 512), F32),
            ((128, 128), F32),
        ],
    )(meta, cot, ext, cot_below, cot_above, wdec, mixed, frame, pre)
    chips, copies = count // 2, lax.axis_size("dp")
    mine, dec = pl.pallas_call(
        reduce_kernel,
        in_specs=[VM],
        out_shape=[shape((27, 128)), shape((27, 64))],
        out_specs=[VM, VM],
        scratch_shapes=[
            pltpu.VMEM((chips, 48, 128), F32),
            pltpu.VMEM((chips, 48, 128), F32),
            pltpu.VMEM((chips, 48, 128), F32),
            pltpu.VMEM((copies, 48, 128), F32),
            pltpu.SemaphoreType.DMA((2,)),
            pltpu.SemaphoreType.DMA((chips,)),
            pltpu.SemaphoreType.DMA((chips,)),
            pltpu.SemaphoreType.DMA((copies,)),
            pltpu.SemaphoreType.DMA((copies,)),
        ],
        compiler_params=pltpu.CompilerParams(
            collective_id=0, has_side_effects=True, vmem_limit_bytes=48 * 1024 * 1024
        ),
    )(coarse.reshape(chips, 2, 48, 128))
    return res.reshape(1, 1, B, 16, 256), mine, dec


def solution(mesh):
    placed = (
        P("dp", "slab", None, None, None, None),
        P("dp", "slab", None, None, None),
        P("dp", "slab", None, None),
        P("dp", "slab", None, None),
        P("dp", "slab", None, None),
        P(),
        P(),
    )
    return jax.shard_map(
        per_device,
        mesh=mesh,
        in_specs=placed,
        out_specs=(P("dp", "slab", None, None, None), P(None, "slab"), P()),
        check_vma=False,
    )
```

```python
import jax
import jax.numpy as jnp
from jax import lax
from jax.experimental import pallas as pl
from jax.experimental.pallas import tpu as pltpu
from jax.sharding import PartitionSpec as P

F32 = jnp.float32
BF16 = jnp.bfloat16
VM = pl.BlockSpec(memory_space=pltpu.VMEM)
SM = pl.BlockSpec(memory_space=pltpu.SMEM)
B = 4


def iota(shape, dim):
    return lax.broadcasted_iota(jnp.int32, shape, dim)


def repeat(count, body, step):
    def some(i, unused):
        for k in range(step):
            body(i * step + k)
        return unused

    if step == count:
        some(0, 0)
    else:
        lax.fori_loop(0, count // step, some, 0)


def lane_roll(v, shift):
    return pltpu.roll(v, shift % 128, v.ndim - 1)


def group_at(dz, dy):
    if dz == 0:
        return 24 * dy
    if dz == 2:
        return 128 + 24 * dy
    return 72 + 24 * dy if dy < 2 else 128 + 72


def pool_phase(feat_ref, pooled_ref):
    row, col = iota((64, 256), 0), iota((64, 256), 1)
    hit = (row // 8 == col // 32) & (row % 8 == (col % 16) // 2)
    gather = jnp.where(hit, 0.125, 0.0).astype(BF16)
    low = iota((64, 128), 1) < 64
    for b in range(B):
        rows = jnp.dot(gather, feat_ref[b].reshape(256, 1024), preferred_element_type=F32)
        for p in range(4):
            first = rows[:, 256 * p : 256 * p + 128]
            second = rows[:, 256 * p + 128 : 256 * p + 256]
            both = jnp.where(low, first + lane_roll(first, 64), second + lane_roll(second, 64))
            both = both.astype(BF16).astype(F32)
            for z in range(8):
                pooled_ref[z, 8 * b : 8 * b + 8, 128 * p : 128 * p + 128] = both[8 * z : 8 * z + 8]


def coarse_weights(wide_ref, band_ref):
    low = iota((64, 128), 1) < 64
    zero = jnp.zeros((64, 128), F32)
    for k in range(9):
        taps = [wide_ref[3 * k + dx].astype(F32) for dx in range(3)]
        for t in range(2):
            for kx in range(8):
                d0 = kx - 1 - 2 * t
                d1 = d0 - 1
                v0 = taps[d0] if 0 <= d0 < 3 else zero
                v1 = taps[d1] if 0 <= d1 < 3 else zero
                band_ref[k, 64 * kx : 64 * kx + 64, 128 * t : 128 * t + 128] = jnp.where(
                    low, v0, v1
                ).astype(BF16)


def pick(link, slots, load):
    v = None
    for a in slots:
        hit = link == a if not isinstance(link, list) else link[a]
        got = load(a)
        v = jnp.where(hit, got, jnp.zeros_like(got) if v is None else v)
    return v


def others(b):
    return [a for a in range(B) if a != b]


def framer(meta, col):
    row = iota((8, 768), 0)

    def masked(cond, v):
        return jnp.where(cond, v, jnp.zeros_like(v))

    def roles(b):
        bx, by = meta[b, 0], meta[b, 1]
        found = {key: [] for key in ((0, 0), (0, 1), (1, 0), (1, 1))}
        for a in range(B):
            ax, ay = meta[a, col], meta[a, col + 1]
            same = (ax >= 0) & (bx >= 0) & ((ax >> 1) == (bx >> 1)) & ((ay >> 1) == (by >> 1))
            for key in found:
                found[key].append(same & ((ax != bx) == bool(key[0])) & ((ay != by) == bool(key[1])))
        return found

    def rows_of(view, who, b):
        xh, yh = meta[b, 0] & 1, meta[b, 1] & 1

        def take(key, lo, hi):
            if col == 0:
                slots = [b] if key == (0, 0) else others(b)
            else:
                slots = list(range(B))
            return pick(who[key], slots, lambda a: view(slice(8 * a, 8 * a + 8), slice(lo, hi)))

        def wide(mid, side):
            return jnp.concatenate(
                [
                    masked(xh == 1, take(side, 384, 512)),
                    take(mid, 0, 512),
                    masked(xh == 0, take(side, 0, 128)),
                ],
                axis=1,
            )

        own = wide((0, 0), (1, 0))
        near = wide((0, 1), (1, 1))
        before = jnp.where(row == 0, masked(yh == 1, pltpu.roll(near, 1, 0)), pltpu.roll(own, 1, 0))
        after = jnp.where(row == 7, masked(yh == 0, pltpu.roll(near, 7, 0)), pltpu.roll(own, 7, 0))
        return before, own, after

    return masked, [roles(b) for b in range(B)], rows_of


def frame_coarse(meta, pooled_ref, frame_ref):
    masked, roles, rows_of = framer(meta, 0)

    def one_plane(z):
        for q in range(2):
            pair = [rows_of(lambda r, c: pooled_ref[z, r, c], roles[b], b) for b in (2 * q, 2 * q + 1)]
            for dy in range(3):
                frame_ref[dy, z + 1, 16 * q : 16 * q + 16, :] = jnp.concatenate(
                    [pair[0][dy], pair[1][dy]], axis=0
                ).astype(BF16)

    repeat(8, one_plane, 2)


def frame_sibling(meta, sib_ref, frame_ref, zh):
    masked, roles, rows_of = framer(meta, 2)
    for q in range(2):
        pair = [rows_of(lambda r, c: sib_ref[r, c], roles[b], b) for b in (2 * q, 2 * q + 1)]
        for dy in range(3):
            both = jnp.concatenate([pair[0][dy], pair[1][dy]], axis=0)
            frame_ref[dy, 0, 16 * q : 16 * q + 16, :] = masked(zh == 1, both).astype(BF16)
            frame_ref[dy, 9, 16 * q : 16 * q + 16, :] = masked(zh == 0, both).astype(BF16)


def coarse_conv(frame_ref, band_ref, pre_ref):
    for h in range(2):
        total = None
        for dz in range(3):
            for dy in range(3):
                lhs = frame_ref[dy, dz : dz + 8, :, 256 * h : 256 * h + 512].reshape(256, 512)
                term = jnp.dot(lhs, band_ref[3 * dz + dy], preferred_element_type=F32)
                total = term if total is None else total + term
        pre_ref[:, :, 256 * h : 256 * h + 256] = total.reshape(8, 32, 256)


def mix_phase(meta, feat_ref, pre_ref, up_ref, mixed_ref, planes):
    low = iota((8, 128), 1) < 64

    def one(zc):
        for b in range(B):
            alive = meta[b, 0] >= 0
            for p in range(4):
                v = pre_ref[zc, 8 * b : 8 * b + 8, 128 * p : 128 * p + 128]
                v = jnp.maximum(v, 0.0).astype(BF16).astype(F32)
                turned = lane_roll(v, 64)
                for half in range(2):
                    d = jnp.where(low, v, turned) if half == 0 else jnp.where(low, turned, v)
                    for r in range(2):
                        up_ref[8 * b + 2 * p + half, pl.ds(r, 8, stride=2), :] = d
            for l in range(8):
                u = up_ref[8 * b + l]
                for r in range(2):
                    f = feat_ref[b, 2 * zc + r, :, 128 * l : 128 * l + 128].astype(F32)
                    m = jnp.where(alive, f + u, 0.0)
                    mixed_ref[b, 2 * zc + r, :, 128 * l : 128 * l + 128] = m.astype(BF16)

    for zc in planes:
        one(zc)


def decoder_bands(wdec_ref, bandt_ref):
    xi = iota((24, 128), 0)
    half = iota((24, 128), 1) // 64
    bandt_ref[...] = jnp.zeros_like(bandt_ref)
    for dz in range(3):
        for dy in range(3):
            taps = [
                jnp.broadcast_to(wdec_ref[9 * dz + 3 * dy + dx : 9 * dz + 3 * dy + dx + 1, :], (24, 128))
                for dx in range(3)
            ]
            at = group_at(dz, dy)
            for l in range(8):
                x = 2 * l + half
                v = jnp.zeros((24, 128), F32)
                for dx in range(3):
                    v = jnp.where(xi == x - dx + 2, taps[dx], v)
                bandt_ref[at : at + 24, 128 * l : 128 * l + 128] = v


def edge_phase(mixed_ref, bandb_ref, edge_ref):
    for side, z, at in ((0, 15, 0), (1, 0, 128)):
        edge = lax.dot_general(
            mixed_ref[:, z].reshape(64, 1024),
            bandb_ref[at : at + 128, :],
            (((1,), (1,)), ((), ())),
            preferred_element_type=F32,
        )
        edge_ref[side] = edge.reshape(B, 16, 128)


def decode_phase(mixed_ref, bandb_ref, tiles_ref, part_ref):
    lane = iota((16, 128), 1)
    bandt = bandb_ref[...]
    for b in range(B):
        tiles = lax.dot_general(
            mixed_ref[b].reshape(256, 1024),
            bandt,
            (((1,), (1,)), ((), ())),
            preferred_element_type=F32,
        )
        tiles_ref[...] = tiles.reshape(16, 16, 256)
        for z in range(16):
            t0, t1 = tiles_ref[z, :, 0:128], tiles_ref[z, :, 128:256]
            v = jnp.where(lane < 48, lane_roll(t0, -72), lane_roll(t1, -24))
            if z > 0:
                v = v + tiles_ref[z - 1, :, 0:128]
            if z < 15:
                v = v + tiles_ref[z + 1, :, 128:256]
            part_ref[256 * b + 16 * z : 256 * b + 16 * z + 16, :] = v


def target_phase(target_ref, wide_ref):
    for y in range(16):
        j, k = y // 8, y % 8
        v = target_ref[:, 128 * j : 128 * j + 128]
        wide_ref[pl.ds(y, 64, stride=16), :] = lane_roll(v, 1 - 16 * k)


def each(planes, body):
    if isinstance(planes, list):
        for z in planes:
            body(z)
    else:
        first, count, step = planes
        repeat(count, lambda i: body(first + i), step)


def plane_at(b, z):
    at = 256 * b + 16 * z
    return pl.ds(at if isinstance(at, int) else pl.multiple_of(at, 16), 16)


def tall_at(b, z, row, rows):
    at = 32 * (18 * b + z) + row
    return pl.ds(at if isinstance(at, int) else pl.multiple_of(at, 8), rows)


def receive_edges(meta, part_ref, edge_ref):
    for b in range(B):
        for i, z in ((0, 0), (1, 15)):
            got = pick(meta[b, 4 + i], range(B), lambda a: edge_ref[i, a])
            part_ref[plane_at(b, z), :] = part_ref[plane_at(b, z), :] + got


def predict_y(meta, part_ref, halo_ref, sum_ref, planes):
    row = iota((16, 128), 0)
    for b in range(B):
        for i, y in ((0, 15), (1, 0)):
            halo_ref[2 * b + i] = pick(
                meta[b, 6 + i], others(b), lambda a: part_ref[pl.ds(256 * a + y, 16, stride=16), :]
            )
    for b in range(B):

        def along_y(z, b=b):
            own = part_ref[plane_at(b, z), :]
            low = jnp.broadcast_to(halo_ref[2 * b, pl.ds(z, 1), :], (16, 128))
            high = jnp.broadcast_to(halo_ref[2 * b + 1, pl.ds(z, 1), :], (16, 128))
            d0 = jnp.where(row == 0, low, pltpu.roll(own, 1, 0))
            d2 = jnp.where(row == 15, high, pltpu.roll(own, 15, 0))
            sum_ref[plane_at(b, z), :] = d0 + lane_roll(own, -24) + lane_roll(d2, -48)

        each(planes, along_y)


def predict_x(meta, sum_ref, wide_ref, res_ref, cot_ref, planes):
    lane = iota((16, 128), 1)
    for b in range(B):

        def along_x(z, b=b):
            at = plane_at(b, z)
            own = sum_ref[at, :]
            low, high = (
                pick(meta[b, 8 + i], others(b), lambda a: sum_ref[plane_at(a, z), :]) for i in range(2)
            )
            own = own + jnp.where(lane == 1, lane_roll(low, -16), 0.0)
            own = own + jnp.where(lane == 16, lane_roll(high, 16), 0.0)
            keep = (lane >= 1) & (lane <= 16) & (meta[b, 0] >= 0)
            res = jnp.where(keep, own - wide_ref[at, :], 0.0)
            res_ref[at, :] = res
            cot_ref[at, :] = (res * (1.0 / 16384)).astype(BF16).astype(F32)

        each(planes, along_x)


def residual_out(res_ref, out_ref):
    group = iota((64, 128), 1) // 16
    for j in range(2):
        v = jnp.zeros((64, 128), F32)
        for k in range(8):
            got = lane_roll(res_ref[pl.ds(8 * j + k, 64, stride=16), :], 16 * k - 1)
            v = jnp.where(group == k, got, v)
        out_ref[:, 128 * j : 128 * j + 128] = v


def spread_x(own, low, high):
    lane = iota(own.shape, 1)
    own = jnp.where(lane == 0, lane_roll(low, -16), own)
    return jnp.where(lane == 17, lane_roll(high, 16), own)


def sides_of(meta, b, load):
    return load(b), *(pick(meta[b, 8 + i], others(b), load) for i in range(2))


ROWS = ((0, 7, 23, 15), (1, 24, 8, 0))


def extend_phase(meta, cot_ref, ext_ref, full_ref, planes):
    for b in range(B):

        def along_x(z, b=b):
            v = spread_x(*sides_of(meta, b, lambda a: cot_ref[plane_at(a, z), :]))
            ext_ref[tall_at(b, z + 1, 8, 16), :] = v
            full_ref[tall_at(b, z + 1, 8, 16), :] = v

        each(planes, along_x)


def extend_rows(meta, ext_ref, spans):
    for b in range(B):
        for i, row, source, _ in ROWS:
            for z, count in spans:
                ext_ref[pl.ds(32 * (18 * b + z) + row, count, stride=32), :] = pick(
                    meta[b, 6 + i],
                    others(b),
                    lambda a: ext_ref[pl.ds(32 * (18 * a + z) + source, count, stride=32), :],
                )


def full_rows(meta, cot_ref, halo_ref, full_ref):
    for b in range(B):
        for i, _, _, y in ROWS:
            halo_ref[2 * b + i] = pick(
                meta[b, 6 + i], others(b), lambda a: cot_ref[pl.ds(256 * a + y, 16, stride=16), :]
            )
    for b in range(B):
        for i, row, _, _ in ROWS:
            v = spread_x(*sides_of(meta, b, lambda a: halo_ref[2 * a + i]))
            full_ref[pl.ds(32 * (18 * b + 1) + row, 16, stride=32), :] = v


def full_edges(meta, cot_in, rim_ref, line_ref, full_ref):
    lane = iota((16, 128), 1)
    for b in range(B):
        for i in range(2):
            got = pick(meta[b, 4 + i], range(B), lambda a: cot_in[i, a].astype(F32))[8:24]
            rim_ref[i, b] = jnp.where((lane >= 1) & (lane <= 16), got, 0.0)
    for b in range(B):
        for i, z in ((0, 0), (1, 17)):
            v = spread_x(*sides_of(meta, b, lambda a: rim_ref[i, a]))
            full_ref[tall_at(b, z, 8, 16), :] = v
            for k, _, _, y in ROWS:
                line_ref[2 * i + k, 8 * b : 8 * b + 8, :] = jnp.broadcast_to(
                    pick(meta[b, 6 + k], others(b), lambda a: rim_ref[i, a, y : y + 1, :]), (8, 128)
                )
    for b in range(B):
        for i, z in ((0, 0), (1, 17)):
            for k, row, _, _ in ROWS:
                v = spread_x(*sides_of(meta, b, lambda a: line_ref[2 * i + k, 8 * a : 8 * a + 8, :]))
                full_ref[tall_at(b, z, row, 1), :] = v[0:1]


def adjoint_taps(ext_ref, taps_ref, planes):
    lane = iota((16, 128), 1)
    for b in range(B):

        def gather(z, b=b):
            s0, s1, s2 = (ext_ref[pl.ds(32 * (18 * b + z) + 9 - dy, 16), :] for dy in range(3))
            taps_ref[b, z] = jnp.where(
                lane < 24, s0, jnp.where(lane < 48, lane_roll(s1, 24), lane_roll(s2, 48))
            )

        each(planes, gather)


def adjoint_place(taps_ref, cat_ref, planes):
    lane = iota((16, 128), 1)
    for b in range(B):

        def place(z, b=b):
            mid = taps_ref[b, z + 1]
            t0 = jnp.where(lane < 72, taps_ref[b, z + 2], lane_roll(mid, 72))
            t1 = jnp.where(lane < 72, taps_ref[b, z], lane_roll(mid, 24))
            cat_ref[b, z] = jnp.concatenate([t0, t1], axis=1).astype(BF16)

        each(planes, place)


def decoder_grad(cat_ref, mixed_ref, cross_ref, out_ref):
    cross_ref[...] = lax.dot_general(
        cat_ref[...].reshape(1024, 256),
        mixed_ref[...].reshape(1024, 1024),
        (((0,), (0,)), ((), ())),
        preferred_element_type=F32,
    )
    xi = iota((24, 128), 0)
    half = iota((24, 128), 1) // 64
    for dz in range(3):
        for dy in range(3):
            at = group_at(dz, dy)
            sums = [jnp.zeros((24, 128), F32) for _ in range(3)]
            for l in range(8):
                v = cross_ref[at : at + 24, 128 * l : 128 * l + 128]
                for dx in range(3):
                    sums[dx] = sums[dx] + jnp.where(xi == 2 * l + half - dx + 2, v, 0.0)
            for dx in range(3):
                line = jnp.sum(sums[dx], axis=0, keepdims=True)
                line = line + lane_roll(line, 64)
                tap = 9 * dz + 3 * dy + dx
                out_ref[tap : tap + 1, :] = line


def spread_gather(full_ref, lhs_ref, planes):
    group = iota((8, 128), 1) // 32
    for z in planes:
        got = []
        for b in range(B):
            v = full_ref[pl.ds(32 * (18 * b + z) + 7, 8, stride=2), :]
            for j in range(1, 4):
                turned = lane_roll(full_ref[pl.ds(32 * (18 * b + z) + 7 + j, 8, stride=2), :], 32 * j)
                v = jnp.where(group == j, turned, v)
            got.append(v)
        p = jnp.concatenate(got, axis=0).astype(BF16)
        for i in range(z % 2, 4, 2):
            zc = (z - i) // 2
            if 0 <= zc < 8:
                lhs_ref[zc, :, 128 * i : 128 * i + 128] = p


def spread_weights(wdec_ref, high_ref, low_ref):
    row, col = iota((64, 32), 0), iota((64, 32), 1)

    def pick(k, d):
        return ((k == 2 - d) | (k == 3 - d)).astype(F32)

    sel = pick(row // 16, col // 9) * pick((row // 4) % 4, (col // 3) % 3) * pick(row % 4, col % 3)
    sel = jnp.where(col < 27, sel, 0.0).astype(BF16)
    summed = jnp.dot(sel, wdec_ref[...].astype(BF16), preferred_element_type=F32)
    x = iota((32, 128), 0)
    half = iota((32, 128), 1) // 64
    for ij in range(16):
        taps = [jnp.broadcast_to(summed[4 * ij + k : 4 * ij + k + 1, :], (32, 128)) for k in range(4)]
        for t in range(4):
            v = jnp.zeros((32, 128), F32)
            for k in range(4):
                v = jnp.where(x - 2 * (2 * t + half) == k, taps[k], v)
            hi = v.astype(BF16)
            high_ref[32 * ij : 32 * ij + 32, 128 * t : 128 * t + 128] = hi
            low_ref[32 * ij : 32 * ij + 32, 128 * t : 128 * t + 128] = (v - hi.astype(F32)).astype(BF16)


def dpre_phase(meta, lhs_ref, high_ref, low_ref, pre_ref, dpre_ref):
    lhs = lhs_ref[...].reshape(256, 512)
    up = jnp.dot(lhs, high_ref[...], preferred_element_type=F32)
    up = up + jnp.dot(lhs, low_ref[...], preferred_element_type=F32)
    up = up.astype(BF16).astype(F32).reshape(8, 32, 512)
    for b in range(B):
        mine = up[:, 8 * b : 8 * b + 8]
        keep = (pre_ref[:, 8 * b : 8 * b + 8] > 0) & (meta[b, 0] >= 0)
        dpre_ref[:, 8 * b : 8 * b + 8] = jnp.where(keep, mine, 0.0)


def turned_halves(dpre_ref):
    dpre = dpre_ref[...].reshape(256, 512)
    return [dpre[:, 256 * h : 256 * h + 256].T.astype(BF16) for h in range(2)]


def coarse_grad(turned, frame_ref, cross_ref, turn_ref, out_ref, dz):
    low = iota((64, 128), 1) < 64
    low16 = iota((16, 128), 1) < 64
    pending = []
    for dy in range(3):
        total = None
        for h in range(2):
            rhs = frame_ref[dy, dz : dz + 8, :, 256 * h : 256 * h + 512].reshape(256, 512)
            term = jnp.dot(turned[h], rhs, preferred_element_type=F32)
            total = term if total is None else total + term
        cross_ref[dy] = total
        for dx in range(3):
            sums = [None, None]
            for n in range(4):
                m = n + dx + 1
                v = cross_ref[dy, 64 * n : 64 * n + 64, 128 * (m // 2) : 128 * (m // 2) + 128]
                sums[m % 2] = v if sums[m % 2] is None else sums[m % 2] + v
            pending.append((3 * dy + dx, sums[0] + lane_roll(sums[1], 64)))
            if len(pending) == 2 or (dy, dx) == (2, 2):
                slot = pending[0][0] % 4 // 2
                first = pending[0][1]
                second = lane_roll(pending[-1][1], 64)
                turn_ref[slot, :, 0:64] = jnp.where(low, first, second).T
                for i, (row, _) in enumerate(pending):
                    for core in range(2):
                        at = 64 * i + 2 * core
                        even = turn_ref[slot, pl.ds(at, 16, stride=4), :]
                        odd = turn_ref[slot, pl.ds(at + 1, 16, stride=4), :]
                        out_ref[dz, core, pl.ds(row, 16, stride=16), :] = jnp.where(
                            low16, even, lane_roll(odd, 64)
                        )
                pending = []


def decoder_rows(dec_ref, local_ref):
    even = dec_ref[pl.ds(0, 16, stride=2), :]
    odd = dec_ref[pl.ds(1, 16, stride=2), :]
    both = jnp.where(iota((16, 128), 1) < 64, even, odd)
    for g, rows in ((0, jnp.zeros((7, 128), F32)), (1, both[0:7]), (2, both[7:14])):
        for core in range(2):
            for k in range(16):
                local_ref[g, core, 16 * k + 9 : 16 * k + 16, :] = rows


def step_kernel(
    meta, feat_hbm, target_ref, wide_ref, wdec_ref,
    out_ref, coarse_ref, dec_out,
    feat_ref, pooled_ref, plane_ref, sib_in, sib_ref, band_ref, frame_ref, pre_ref, up_ref, mixed_ref,
    bandt_ref, bandb_ref, tiles_ref, part_ref, edge_out, edge_in, cot_out, cot_in, spot_ref, sum_ref,
    cot_ref, res_ref, ext_ref, taps_ref, cat_ref, dcross_ref, halo_ref, rim_ref, line_ref, full_ref, lhs_ref, high_ref,
    low_ref, dpre_ref, cross_ref, turn_ref, dec_ref, local_ref, mate_ref, half_ref, chips_ref, parts_ref,
    feat_sems, sib_sems, edge_sends, edge_recvs, cot_sends, cot_recvs, mate_sends, mate_recvs,
    chip_sends, chip_recvs, dp_sends, dp_recvs,
):
    slab, dp = lax.axis_index("slab"), lax.axis_index("dp")
    count = lax.axis_size("slab")
    core, chip = slab % 2, slab // 2
    chips, copies = count // 2, lax.axis_size("dp")
    sibling = {"slab": slab + 1 - 2 * core}
    around = [{"slab": lax.rem(slab + 1, count)}, {"slab": lax.rem(slab + count - 1, count)}]

    def peer(r):
        return lax.rem(chip + r, chips)

    def twin(r):
        return lax.rem(dp + r, copies)

    def remote(src, dst, send, recv, device):
        return pltpu.make_async_remote_copy(
            src_ref=src,
            dst_ref=dst,
            send_sem=send,
            recv_sem=recv,
            device_id=device,
            device_id_type=pl.DeviceIdType.MESH,
        )

    barrier = pltpu.get_barrier_semaphore()
    greeted = around + [{"slab": 2 * peer(r) + core} for r in range(1, chips)]
    greeted = greeted + [{"dp": twin(r)} for r in range(1, copies)]
    for device in greeted:
        pl.semaphore_signal(barrier, inc=1, device_id=device, device_id_type=pl.DeviceIdType.MESH)

    loads = [
        pltpu.make_async_copy(feat_hbm.at[b], feat_ref.at[b], feat_sems.at[b]) for b in range(B)
    ]
    for load in loads:
        load.start()
    coarse_weights(wide_ref, band_ref)
    for load in loads:
        load.wait()
    pool_phase(feat_ref, pooled_ref)
    plane_ref[...] = pooled_ref[7 * (1 - core)].astype(BF16)
    pl.semaphore_wait(barrier, len(greeted))
    swap = remote(plane_ref, sib_in, sib_sems.at[0], sib_sems.at[1], sibling)
    swap.start()
    frame_coarse(meta, pooled_ref, frame_ref)
    decoder_bands(wdec_ref, bandt_ref)
    bandb_ref[...] = bandt_ref[...].astype(BF16)
    swap.wait()
    sib_ref[...] = sib_in[...].astype(F32)
    frame_sibling(meta, sib_ref, frame_ref, core)
    coarse_conv(frame_ref, band_ref, pre_ref)

    mix_phase(meta, feat_ref, pre_ref, up_ref, mixed_ref, [0, 7])
    edge_phase(mixed_ref, bandb_ref, edge_out)
    edges = [
        remote(edge_out.at[i], edge_in.at[i], edge_sends.at[i], edge_recvs.at[i], around[i])
        for i in range(2)
    ]
    for copy in edges:
        copy.start()
    mix_phase(meta, feat_ref, pre_ref, up_ref, mixed_ref, [1, 2, 3, 4, 5, 6])
    decode_phase(mixed_ref, bandb_ref, tiles_ref, part_ref)
    target_phase(target_ref, spot_ref)
    inner = (1, 14, 7)
    predict_y(meta, part_ref, halo_ref, sum_ref, inner)
    for copy in edges:
        copy.wait()
    receive_edges(meta, part_ref, edge_in)
    predict_y(meta, part_ref, halo_ref, sum_ref, [0, 15])
    predict_x(meta, sum_ref, spot_ref, res_ref, cot_ref, [0, 15])
    extend_phase(meta, cot_ref, ext_ref, full_ref, [0, 15])
    extend_rows(meta, ext_ref, [(1, 1), (16, 1)])
    for b in range(B):
        cot_out[0, b] = ext_ref[tall_at(b, 16, 0, 32), :].astype(BF16)
        cot_out[1, b] = ext_ref[tall_at(b, 1, 0, 32), :].astype(BF16)
    sides = [
        remote(cot_out.at[i], cot_in.at[i], cot_sends.at[i], cot_recvs.at[i], around[i])
        for i in range(2)
    ]
    for copy in sides:
        copy.start()
    predict_x(meta, sum_ref, spot_ref, res_ref, cot_ref, inner)
    extend_phase(meta, cot_ref, ext_ref, full_ref, inner)
    full_rows(meta, cot_ref, halo_ref, full_ref)
    spread_gather(full_ref, lhs_ref, list(range(1, 17)))
    spread_weights(wdec_ref, high_ref, low_ref)
    extend_rows(meta, ext_ref, [(2, 14)])
    adjoint_taps(ext_ref, taps_ref, (1, 16, 8))
    adjoint_place(taps_ref, cat_ref, inner)
    residual_out(res_ref, out_ref)
    for copy in sides:
        copy.wait()
    full_edges(meta, cot_in, rim_ref, line_ref, full_ref)
    spread_gather(full_ref, lhs_ref, [0, 17])
    dpre_phase(meta, lhs_ref, high_ref, low_ref, pre_ref, dpre_ref)
    turned = turned_halves(dpre_ref)

    mates = [
        remote(local_ref.at[g, 1 - core], mate_ref.at[g], mate_sends.at[g], mate_recvs.at[g], sibling)
        for g in range(3)
    ]

    def to_chip(g, r):
        return remote(
            half_ref.at[g, peer(r)], chips_ref.at[g, chip],
            chip_sends.at[g, r], chip_recvs.at[g, chip], {"slab": 2 * peer(r) + core},
        )

    def from_chip(g, r):
        return remote(
            half_ref.at[g, chip], chips_ref.at[g, peer(r)],
            chip_sends.at[g, r], chip_recvs.at[g, peer(r)], {"slab": 2 * peer(r) + core},
        )

    def send_out(g):
        mates[g].wait_recv()
        half_ref[g] = (local_ref[g, core] + mate_ref[g]).reshape(chips, 16, 128)
        for r in range(1, chips):
            to_chip(g, r).start()
        chips_ref[g, chip] = half_ref[g, chip]

    def collect(g):
        for r in range(1, chips):
            from_chip(g, r).wait_recv()
        total = chips_ref[g, 0]
        for k in range(1, chips):
            total = total + chips_ref[g, k]
        parts_ref[dp, 16 * g : 16 * g + 16, :] = total

    for b in range(B):
        for i, z in ((0, 0), (1, 17)):
            got = pick(meta[b, 4 + i], range(B), lambda a: cot_in[i, a].astype(F32))
            ext_ref[tall_at(b, z, 0, 32), :] = got
    adjoint_taps(ext_ref, taps_ref, [0, 17])
    adjoint_place(taps_ref, cat_ref, [0, 15])
    decoder_grad(cat_ref, mixed_ref, dcross_ref, dec_ref)
    decoder_rows(dec_ref, local_ref)
    for g in range(3):
        coarse_grad(turned, frame_ref, cross_ref, turn_ref, local_ref, g)
        mates[g].start()
        if g > 0:
            send_out(g - 1)
    send_out(2)
    for g in range(3):
        collect(g)

    def to_twin(r):
        return remote(
            parts_ref.at[dp], parts_ref.at[dp], dp_sends.at[r], dp_recvs.at[dp], {"dp": twin(r)}
        )

    def from_twin(r):
        return remote(
            parts_ref.at[dp], parts_ref.at[twin(r)], dp_sends.at[r], dp_recvs.at[twin(r)], {"dp": twin(r)}
        )

    for r in range(1, copies):
        to_twin(r).start()
    for r in range(1, copies):
        from_twin(r).wait_recv()
    total = parts_ref[0]
    for k in range(1, copies):
        total = total + parts_ref[k]
    for g in range(3):
        coarse_ref[9 * g : 9 * g + 9, :] = total[16 * g : 16 * g + 9]
    for tap in range(27):
        at = 25 + tap // 2 if tap < 14 else 41 + tap // 2 - 7
        dec_out[tap : tap + 1, :] = total[at : at + 1, 64 * (tap % 2) : 64 * (tap % 2) + 64]
    for g in range(3):
        mates[g].wait_send()
        for r in range(1, chips):
            to_chip(g, r).wait_send()
    for r in range(1, copies):
        to_twin(r).wait_send()


def shape(dims, dtype=F32):
    return jax.ShapeDtypeStruct(dims, dtype)


def per_device(features, target, block_coords, neighbours, owners, coarse_weight, decoder_weight):
    coords = block_coords[0, 0]
    slab, count, copies = lax.axis_index("slab"), lax.axis_size("slab"), lax.axis_size("dp")
    chips = count // 2
    sib_coords = lax.ppermute(coords, "slab", [(i, i ^ 1) for i in range(count)])
    side = jnp.arange(6, dtype=jnp.int32)[None, :]
    outside = ((side == 0) & (slab == 0)) | ((side == 1) & (slab == count - 1))
    links = jnp.where(outside, -1, neighbours[0, 0])
    meta = jnp.concatenate([coords, sib_coords, links], axis=1)
    w3 = coarse_weight.reshape(27, 64, 64)
    wide = jnp.concatenate([w3, w3], axis=2)
    wdec = jnp.pad(
        jnp.concatenate([decoder_weight, decoder_weight], axis=1).astype(F32), ((0, 5), (0, 0))
    )
    scratch = [
        ((B, 16, 16, 1024), BF16),
        ((8, 32, 512), F32),
        ((32, 512), BF16),
        ((32, 512), BF16),
        ((32, 512), F32),
        ((9, 512, 256), BF16),
        ((3, 10, 32, 768), BF16),
        ((8, 32, 512), F32),
        ((32, 16, 128), F32),
        ((B, 16, 16, 1024), BF16),
        ((256, 1024), F32),
        ((256, 1024), BF16),
        ((16, 16, 256), F32),
        ((1024, 128), F32),
        ((2, B, 16, 128), F32),
        ((2, B, 16, 128), F32),
        ((2, B, 32, 128), BF16),
        ((2, B, 32, 128), BF16),
        ((1024, 128), F32),
        ((1024, 128), F32),
        ((1024, 128), F32),
        ((1024, 128), F32),
        ((B * 18 * 32, 128), F32),
        ((B, 18, 16, 128), F32),
        ((B, 16, 16, 256), BF16),
        ((256, 1024), F32),
        ((2 * B, 16, 128), F32),
        ((2, B, 16, 128), F32),
        ((4, 8 * B, 128), F32),
        ((B * 18 * 32, 128), F32),
        ((8, 32, 512), BF16),
        ((512, 512), BF16),
        ((512, 512), BF16),
        ((8, 32, 512), F32),
        ((3, 256, 512), F32),
        ((2, 128, 128), F32),
        ((32, 128), F32),
        ((3, 2, 256, 128), F32),
        ((3, 256, 128), F32),
        ((3, chips, 16, 128), F32),
        ((3, chips, 16, 128), F32),
        ((copies, 48, 128), F32),
    ]
    sems = [(B,), (2,), (2,), (2,), (2,), (2,), (3,), (3,), (3, chips), (3, chips), (copies,), (copies,)]
    res, mine, dec = pl.pallas_call(
        step_kernel,
        in_specs=[SM, pl.BlockSpec(memory_space=pl.ANY), VM, VM, VM],
        out_shape=[shape((64, 256)), shape((27, 128)), shape((27, 64))],
        out_specs=[VM, VM, VM],
        scratch_shapes=[pltpu.VMEM(d, t) for d, t in scratch]
        + [pltpu.SemaphoreType.DMA(d) for d in sems],
        compiler_params=pltpu.CompilerParams(
            collective_id=0, has_side_effects=True, vmem_limit_bytes=48 * 1024 * 1024
        ),
    )(meta, features[0, 0], target[0, 0].reshape(64, 256), wide, wdec)
    return res.reshape(1, 1, B, 16, 256), mine, dec


def solution(mesh):
    placed = (
        P("dp", "slab", None, None, None, None),
        P("dp", "slab", None, None, None),
        P("dp", "slab", None, None),
        P("dp", "slab", None, None),
        P("dp", "slab", None, None),
        P(),
        P(),
    )
    return jax.shard_map(
        per_device,
        mesh=mesh,
        in_specs=placed,
        out_specs=(P("dp", "slab", None, None, None), P(None, "slab"), P()),
        check_vma=False,
    )
```

```python
import jax
import jax.numpy as jnp
from jax import lax
from jax.experimental import pallas as pl
from jax.experimental.pallas import tpu as pltpu
from jax.sharding import PartitionSpec as P

F32 = jnp.float32
BF16 = jnp.bfloat16
VM = pl.BlockSpec(memory_space=pltpu.VMEM)
SM = pl.BlockSpec(memory_space=pltpu.SMEM)
ANY = pl.BlockSpec(memory_space=pl.ANY)
B = 4


def iota(shape, dim):
    return lax.broadcasted_iota(jnp.int32, shape, dim)


def repeat(count, body, step):
    def some(i, unused):
        for k in range(step):
            body(i * step + k)
        return unused

    if step == count:
        some(0, 0)
    else:
        lax.fori_loop(0, count // step, some, 0)


def lane_roll(v, shift):
    return pltpu.roll(v, shift % 128, v.ndim - 1)


def group_at(dz, dy):
    if dz == 0:
        return 24 * dy
    if dz == 2:
        return 128 + 24 * dy
    return 72 + 24 * dy if dy < 2 else 128 + 72


class Meta:
    def __init__(self, coords, links, slab, count):
        self.coords, self.links = coords, links
        self.ends = {4: slab == 0, 5: slab == count - 1}

    def __getitem__(self, at):
        b, col = at
        if col < 4:
            return self.coords[col, b]
        link = self.links[b, col - 4]
        return jnp.where(self.ends[col], -1, link) if col in self.ends else link


def widen_weights(cw_ref, dw_ref, wide_ref, wdec_ref):
    low = iota((27, 128), 1) < 64
    for t in range(32):
        v = cw_ref[:, 128 * t : 128 * t + 128].astype(F32)
        turned = lane_roll(v, 64)
        wide_ref[pl.ds(2 * t, 27, stride=64), :] = jnp.where(low, v, turned)
        wide_ref[pl.ds(2 * t + 1, 27, stride=64), :] = jnp.where(low, turned, v)
    w = dw_ref[...].astype(F32)
    wdec_ref[...] = jnp.zeros_like(wdec_ref)
    wdec_ref[0:27, 0:64] = w
    wdec_ref[0:27, 64:128] = w


def pool_phase(feat_ref, pooled_ref, loads):
    row, col = iota((64, 256), 0), iota((64, 256), 1)
    hit = (row // 8 == col // 32) & (row % 8 == (col % 16) // 2)
    gather = jnp.where(hit, 0.125, 0.0).astype(BF16)
    low = iota((64, 128), 1) < 64
    for b in range(B):
        loads[b].wait()
        rows = jnp.dot(gather, feat_ref[b].reshape(256, 1024), preferred_element_type=F32)
        for p in range(4):
            first = rows[:, 256 * p : 256 * p + 128]
            second = rows[:, 256 * p + 128 : 256 * p + 256]
            both = jnp.where(low, first + lane_roll(first, 64), second + lane_roll(second, 64))
            both = both.astype(BF16).astype(F32)
            for z in range(8):
                pooled_ref[z, 8 * b : 8 * b + 8, 128 * p : 128 * p + 128] = both[8 * z : 8 * z + 8]


def coarse_weights(wide_ref, band_ref):
    low = iota((64, 128), 1) < 64
    zero = jnp.zeros((64, 128), F32)
    for k in range(9):
        taps = [wide_ref[64 * (3 * k + dx) : 64 * (3 * k + dx) + 64, :] for dx in range(3)]
        for t in range(2):
            for kx in range(8):
                d0 = kx - 1 - 2 * t
                d1 = d0 - 1
                v0 = taps[d0] if 0 <= d0 < 3 else zero
                v1 = taps[d1] if 0 <= d1 < 3 else zero
                band_ref[k, 64 * kx : 64 * kx + 64, 128 * t : 128 * t + 128] = jnp.where(
                    low, v0, v1
                ).astype(BF16)


def pick(link, slots, load):
    v = None
    for a in slots:
        hit = link == a if not isinstance(link, list) else link[a]
        got = load(a)
        v = jnp.where(hit, got, jnp.zeros_like(got) if v is None else v)
    return v


def others(b):
    return [a for a in range(B) if a != b]


def framer(meta, spots=None):
    row = iota((8, 768), 0)

    def masked(cond, v):
        return jnp.where(cond, v, jnp.zeros_like(v))

    def roles(b):
        bx, by = meta[b, 0], meta[b, 1]
        found = {key: [] for key in ((0, 0), (0, 1), (1, 0), (1, 1))}
        for a in range(B):
            if spots is None:
                ax, ay = meta[a, 0], meta[a, 1]
            else:
                ax, ay = (
                    jnp.broadcast_to(spots[B * i + a : B * i + a + 1, :], (8, 128)) for i in range(2)
                )
            same = (ax >= 0) & (bx >= 0) & ((ax >> 1) == (bx >> 1)) & ((ay >> 1) == (by >> 1))
            for key in found:
                off_x = ax != bx if key[0] else ax == bx
                off_y = ay != by if key[1] else ay == by
                found[key].append(same & off_x & off_y)
        return found

    def rows_of(view, who, b):
        xh, yh = meta[b, 0] & 1, meta[b, 1] & 1

        def take(key, lo, hi):
            if spots is None:
                slots = [b] if key == (0, 0) else others(b)
                return pick(who[key], slots, lambda a: view(slice(8 * a, 8 * a + 8), slice(lo, hi)))
            parts = [
                pick(who[key], range(B), lambda a: view(slice(8 * a, 8 * a + 8), slice(at, at + 128)))
                for at in range(lo, hi, 128)
            ]
            return parts[0] if len(parts) == 1 else jnp.concatenate(parts, axis=1)

        def wide(mid, side):
            return jnp.concatenate(
                [
                    masked(xh == 1, take(side, 384, 512)),
                    take(mid, 0, 512),
                    masked(xh == 0, take(side, 0, 128)),
                ],
                axis=1,
            )

        own = wide((0, 0), (1, 0))
        near = wide((0, 1), (1, 1))
        before = jnp.where(row == 0, masked(yh == 1, pltpu.roll(near, 1, 0)), pltpu.roll(own, 1, 0))
        after = jnp.where(row == 7, masked(yh == 0, pltpu.roll(near, 7, 0)), pltpu.roll(own, 7, 0))
        return before, own, after

    return masked, [roles(b) for b in range(B)], rows_of


def frame_coarse(meta, pooled_ref, frame_ref):
    masked, roles, rows_of = framer(meta)

    def one_plane(z):
        for q in range(2):
            pair = [rows_of(lambda r, c: pooled_ref[z, r, c], roles[b], b) for b in (2 * q, 2 * q + 1)]
            for dy in range(3):
                frame_ref[dy, z + 1, 16 * q : 16 * q + 16, :] = jnp.concatenate(
                    [pair[0][dy], pair[1][dy]], axis=0
                ).astype(BF16)

    repeat(8, one_plane, 2)


def frame_sibling(meta, spots, sib_ref, frame_ref, zh):
    masked, roles, rows_of = framer(meta, spots)
    for q in range(2):
        pair = [rows_of(lambda r, c: sib_ref[r, c], roles[b], b) for b in (2 * q, 2 * q + 1)]
        for dy in range(3):
            both = jnp.concatenate([pair[0][dy], pair[1][dy]], axis=0)
            frame_ref[dy, 0, 16 * q : 16 * q + 16, :] = masked(zh == 1, both).astype(BF16)
            frame_ref[dy, 9, 16 * q : 16 * q + 16, :] = masked(zh == 0, both).astype(BF16)


def coarse_conv(frame_ref, band_ref, pre_ref):
    for h in range(2):
        total = None
        for dz in range(3):
            for dy in range(3):
                lhs = frame_ref[dy, dz : dz + 8, :, 256 * h : 256 * h + 512].reshape(256, 512)
                term = jnp.dot(lhs, band_ref[3 * dz + dy], preferred_element_type=F32)
                total = term if total is None else total + term
        pre_ref[:, :, 256 * h : 256 * h + 256] = total.reshape(8, 32, 256)


def mix_phase(meta, feat_ref, pre_ref, up_ref, mixed_ref, planes):
    low = iota((8, 128), 1) < 64

    def one(zc):
        for b in range(B):
            alive = meta[b, 0] >= 0
            for p in range(4):
                v = pre_ref[zc, 8 * b : 8 * b + 8, 128 * p : 128 * p + 128]
                v = jnp.maximum(v, 0.0).astype(BF16).astype(F32)
                turned = lane_roll(v, 64)
                for half in range(2):
                    d = jnp.where(low, v, turned) if half == 0 else jnp.where(low, turned, v)
                    for r in range(2):
                        up_ref[8 * b + 2 * p + half, pl.ds(r, 8, stride=2), :] = d
            for l in range(8):
                u = up_ref[8 * b + l]
                for r in range(2):
                    f = feat_ref[b, 2 * zc + r, :, 128 * l : 128 * l + 128].astype(F32)
                    m = jnp.where(alive, f + u, 0.0)
                    mixed_ref[b, 2 * zc + r, :, 128 * l : 128 * l + 128] = m.astype(BF16)

    for zc in planes:
        one(zc)


def decoder_bands(wdec_ref, bandt_ref):
    xi = iota((24, 128), 0)
    half = iota((24, 128), 1) // 64
    bandt_ref[...] = jnp.zeros_like(bandt_ref)
    for dz in range(3):
        for dy in range(3):
            taps = [
                jnp.broadcast_to(wdec_ref[9 * dz + 3 * dy + dx : 9 * dz + 3 * dy + dx + 1, :], (24, 128))
                for dx in range(3)
            ]
            at = group_at(dz, dy)
            for l in range(8):
                x = 2 * l + half
                v = jnp.zeros((24, 128), F32)
                for dx in range(3):
                    v = jnp.where(xi == x - dx + 2, taps[dx], v)
                bandt_ref[at : at + 24, 128 * l : 128 * l + 128] = v


def edge_phase(mixed_ref, bandb_ref, edge_ref):
    for side, z, at in ((0, 15, 0), (1, 0, 128)):
        edge = lax.dot_general(
            mixed_ref[:, z].reshape(64, 1024),
            bandb_ref[at : at + 128, :],
            (((1,), (1,)), ((), ())),
            preferred_element_type=F32,
        )
        edge_ref[side] = edge.reshape(B, 16, 128)


def decode_phase(mixed_ref, bandb_ref, tiles_ref, part_ref):
    lane = iota((16, 128), 1)
    bandt = bandb_ref[...]
    for b in range(B):
        tiles = lax.dot_general(
            mixed_ref[b].reshape(256, 1024),
            bandt,
            (((1,), (1,)), ((), ())),
            preferred_element_type=F32,
        )
        tiles_ref[...] = tiles.reshape(16, 16, 256)
        for z in range(16):
            t0, t1 = tiles_ref[z, :, 0:128], tiles_ref[z, :, 128:256]
            v = jnp.where(lane < 48, lane_roll(t0, -72), lane_roll(t1, -24))
            if z > 0:
                v = v + tiles_ref[z - 1, :, 0:128]
            if z < 15:
                v = v + tiles_ref[z + 1, :, 128:256]
            part_ref[256 * b + 16 * z : 256 * b + 16 * z + 16, :] = v


def target_phase(target_ref, wide_ref):
    for y in range(16):
        j, k = y // 8, y % 8
        v = target_ref[:, 128 * j : 128 * j + 128]
        wide_ref[pl.ds(y, 64, stride=16), :] = lane_roll(v, 1 - 16 * k)


def each(planes, body):
    if isinstance(planes, list):
        for z in planes:
            body(z)
    else:
        first, count, step = planes
        repeat(count, lambda i: body(first + i), step)


def plane_at(b, z):
    at = 256 * b + 16 * z
    return pl.ds(at if isinstance(at, int) else pl.multiple_of(at, 16), 16)


def tall_at(b, z, row, rows):
    at = 32 * (18 * b + z) + row
    return pl.ds(at if isinstance(at, int) else pl.multiple_of(at, 8), rows)


def receive_edges(meta, part_ref, edge_ref):
    for b in range(B):
        for i, z in ((0, 0), (1, 15)):
            got = pick(meta[b, 4 + i], range(B), lambda a: edge_ref[i, a])
            part_ref[plane_at(b, z), :] = part_ref[plane_at(b, z), :] + got


def predict_y(meta, part_ref, halo_ref, sum_ref, planes):
    row = iota((16, 128), 0)
    for b in range(B):
        for i, y in ((0, 15), (1, 0)):
            halo_ref[2 * b + i] = pick(
                meta[b, 6 + i], others(b), lambda a: part_ref[pl.ds(256 * a + y, 16, stride=16), :]
            )
    for b in range(B):

        def along_y(z, b=b):
            own = part_ref[plane_at(b, z), :]
            low = jnp.broadcast_to(halo_ref[2 * b, pl.ds(z, 1), :], (16, 128))
            high = jnp.broadcast_to(halo_ref[2 * b + 1, pl.ds(z, 1), :], (16, 128))
            d0 = jnp.where(row == 0, low, pltpu.roll(own, 1, 0))
            d2 = jnp.where(row == 15, high, pltpu.roll(own, 15, 0))
            sum_ref[plane_at(b, z), :] = d0 + lane_roll(own, -24) + lane_roll(d2, -48)

        each(planes, along_y)


def predict_x(meta, sum_ref, wide_ref, res_ref, cot_ref, planes):
    lane = iota((16, 128), 1)
    for b in range(B):

        def along_x(z, b=b):
            at = plane_at(b, z)
            own = sum_ref[at, :]
            low, high = (
                pick(meta[b, 8 + i], others(b), lambda a: sum_ref[plane_at(a, z), :]) for i in range(2)
            )
            own = own + jnp.where(lane == 1, lane_roll(low, -16), 0.0)
            own = own + jnp.where(lane == 16, lane_roll(high, 16), 0.0)
            keep = (lane >= 1) & (lane <= 16) & (meta[b, 0] >= 0)
            res = jnp.where(keep, own - wide_ref[at, :], 0.0)
            res_ref[at, :] = res
            cot_ref[at, :] = (res * (1.0 / 16384)).astype(BF16).astype(F32)

        each(planes, along_x)


def residual_out(res_ref, out_ref):
    group = iota((64, 128), 1) // 16
    for j in range(2):
        v = jnp.zeros((64, 128), F32)
        for k in range(8):
            got = lane_roll(res_ref[pl.ds(8 * j + k, 64, stride=16), :], 16 * k - 1)
            v = jnp.where(group == k, got, v)
        out_ref[:, 128 * j : 128 * j + 128] = v


def spread_x(own, low, high):
    lane = iota(own.shape, 1)
    own = jnp.where(lane == 0, lane_roll(low, -16), own)
    return jnp.where(lane == 17, lane_roll(high, 16), own)


def sides_of(meta, b, load):
    return load(b), *(pick(meta[b, 8 + i], others(b), load) for i in range(2))


ROWS = ((0, 7, 23, 15), (1, 24, 8, 0))


def extend_phase(meta, cot_ref, ext_ref, full_ref, planes):
    for b in range(B):

        def along_x(z, b=b):
            v = spread_x(*sides_of(meta, b, lambda a: cot_ref[plane_at(a, z), :]))
            ext_ref[tall_at(b, z + 1, 8, 16), :] = v
            full_ref[tall_at(b, z + 1, 8, 16), :] = v

        each(planes, along_x)


def extend_rows(meta, ext_ref, spans):
    for b in range(B):
        for i, row, source, _ in ROWS:
            for z, count in spans:
                ext_ref[pl.ds(32 * (18 * b + z) + row, count, stride=32), :] = pick(
                    meta[b, 6 + i],
                    others(b),
                    lambda a: ext_ref[pl.ds(32 * (18 * a + z) + source, count, stride=32), :],
                )


def full_rows(meta, cot_ref, halo_ref, full_ref):
    for b in range(B):
        for i, _, _, y in ROWS:
            halo_ref[2 * b + i] = pick(
                meta[b, 6 + i], others(b), lambda a: cot_ref[pl.ds(256 * a + y, 16, stride=16), :]
            )
    for b in range(B):
        for i, row, _, _ in ROWS:
            v = spread_x(*sides_of(meta, b, lambda a: halo_ref[2 * a + i]))
            full_ref[pl.ds(32 * (18 * b + 1) + row, 16, stride=32), :] = v


def full_edges(meta, cot_in, rim_ref, line_ref, full_ref):
    lane = iota((16, 128), 1)
    for b in range(B):
        for i in range(2):
            got = pick(meta[b, 4 + i], range(B), lambda a: cot_in[i, a].astype(F32))[8:24]
            rim_ref[i, b] = jnp.where((lane >= 1) & (lane <= 16), got, 0.0)
    for b in range(B):
        for i, z in ((0, 0), (1, 17)):
            v = spread_x(*sides_of(meta, b, lambda a: rim_ref[i, a]))
            full_ref[tall_at(b, z, 8, 16), :] = v
            for k, _, _, y in ROWS:
                line_ref[2 * i + k, 8 * b : 8 * b + 8, :] = jnp.broadcast_to(
                    pick(meta[b, 6 + k], others(b), lambda a: rim_ref[i, a, y : y + 1, :]), (8, 128)
                )
    for b in range(B):
        for i, z in ((0, 0), (1, 17)):
            for k, row, _, _ in ROWS:
                v = spread_x(*sides_of(meta, b, lambda a: line_ref[2 * i + k, 8 * a : 8 * a + 8, :]))
                full_ref[tall_at(b, z, row, 1), :] = v[0:1]


def adjoint_taps(ext_ref, taps_ref, planes):
    lane = iota((16, 128), 1)
    for b in range(B):

        def gather(z, b=b):
            s0, s1, s2 = (ext_ref[pl.ds(32 * (18 * b + z) + 9 - dy, 16), :] for dy in range(3))
            taps_ref[b, z] = jnp.where(
                lane < 24, s0, jnp.where(lane < 48, lane_roll(s1, 24), lane_roll(s2, 48))
            )

        each(planes, gather)


def adjoint_place(taps_ref, cat_ref, planes):
    lane = iota((16, 128), 1)
    for b in range(B):

        def place(z, b=b):
            mid = taps_ref[b, z + 1]
            t0 = jnp.where(lane < 72, taps_ref[b, z + 2], lane_roll(mid, 72))
            t1 = jnp.where(lane < 72, taps_ref[b, z], lane_roll(mid, 24))
            cat_ref[b, z] = jnp.concatenate([t0, t1], axis=1).astype(BF16)

        each(planes, place)


def decoder_grad(cat_ref, mixed_ref, cross_ref, out_ref):
    cross_ref[...] = lax.dot_general(
        cat_ref[...].reshape(1024, 256),
        mixed_ref[...].reshape(1024, 1024),
        (((0,), (0,)), ((), ())),
        preferred_element_type=F32,
    )
    xi = iota((24, 128), 0)
    half = iota((24, 128), 1) // 64
    for dz in range(3):
        for dy in range(3):
            at = group_at(dz, dy)
            sums = [jnp.zeros((24, 128), F32) for _ in range(3)]
            for l in range(8):
                v = cross_ref[at : at + 24, 128 * l : 128 * l + 128]
                for dx in range(3):
                    sums[dx] = sums[dx] + jnp.where(xi == 2 * l + half - dx + 2, v, 0.0)
            for dx in range(3):
                line = jnp.sum(sums[dx], axis=0, keepdims=True)
                line = line + lane_roll(line, 64)
                tap = 9 * dz + 3 * dy + dx
                out_ref[tap : tap + 1, :] = line


def spread_gather(full_ref, lhs_ref, planes):
    group = iota((8, 128), 1) // 32
    for z in planes:
        got = []
        for b in range(B):
            v = full_ref[pl.ds(32 * (18 * b + z) + 7, 8, stride=2), :]
            for j in range(1, 4):
                turned = lane_roll(full_ref[pl.ds(32 * (18 * b + z) + 7 + j, 8, stride=2), :], 32 * j)
                v = jnp.where(group == j, turned, v)
            got.append(v)
        p = jnp.concatenate(got, axis=0).astype(BF16)
        for i in range(z % 2, 4, 2):
            zc = (z - i) // 2
            if 0 <= zc < 8:
                lhs_ref[zc, :, 128 * i : 128 * i + 128] = p


def spread_weights(wdec_ref, high_ref, low_ref):
    row, col = iota((64, 32), 0), iota((64, 32), 1)

    def pick(k, d):
        return ((k == 2 - d) | (k == 3 - d)).astype(F32)

    sel = pick(row // 16, col // 9) * pick((row // 4) % 4, (col // 3) % 3) * pick(row % 4, col % 3)
    sel = jnp.where(col < 27, sel, 0.0).astype(BF16)
    summed = jnp.dot(sel, wdec_ref[...].astype(BF16), preferred_element_type=F32)
    x = iota((32, 128), 0)
    half = iota((32, 128), 1) // 64
    for ij in range(16):
        taps = [jnp.broadcast_to(summed[4 * ij + k : 4 * ij + k + 1, :], (32, 128)) for k in range(4)]
        for t in range(4):
            v = jnp.zeros((32, 128), F32)
            for k in range(4):
                v = jnp.where(x - 2 * (2 * t + half) == k, taps[k], v)
            hi = v.astype(BF16)
            high_ref[32 * ij : 32 * ij + 32, 128 * t : 128 * t + 128] = hi
            low_ref[32 * ij : 32 * ij + 32, 128 * t : 128 * t + 128] = (v - hi.astype(F32)).astype(BF16)


def dpre_phase(meta, lhs_ref, high_ref, low_ref, pre_ref, dpre_ref):
    lhs = lhs_ref[...].reshape(256, 512)
    up = jnp.dot(lhs, high_ref[...], preferred_element_type=F32)
    up = up + jnp.dot(lhs, low_ref[...], preferred_element_type=F32)
    up = up.astype(BF16).astype(F32).reshape(8, 32, 512)
    for b in range(B):
        mine = up[:, 8 * b : 8 * b + 8]
        keep = (pre_ref[:, 8 * b : 8 * b + 8] > 0) & (meta[b, 0] >= 0)
        dpre_ref[:, 8 * b : 8 * b + 8] = jnp.where(keep, mine, 0.0)


def turned_halves(dpre_ref):
    dpre = dpre_ref[...].reshape(256, 512)
    return [dpre[:, 256 * h : 256 * h + 256].T.astype(BF16) for h in range(2)]


def coarse_grad(turned, frame_ref, cross_ref, turn_ref, out_ref, dz):
    low = iota((64, 128), 1) < 64
    low16 = iota((16, 128), 1) < 64
    pending = []
    for dy in range(3):
        total = None
        for h in range(2):
            rhs = frame_ref[dy, dz : dz + 8, :, 256 * h : 256 * h + 512].reshape(256, 512)
            term = jnp.dot(turned[h], rhs, preferred_element_type=F32)
            total = term if total is None else total + term
        cross_ref[dy] = total
        for dx in range(3):
            sums = [None, None]
            for n in range(4):
                m = n + dx + 1
                v = cross_ref[dy, 64 * n : 64 * n + 64, 128 * (m // 2) : 128 * (m // 2) + 128]
                sums[m % 2] = v if sums[m % 2] is None else sums[m % 2] + v
            pending.append((3 * dy + dx, sums[0] + lane_roll(sums[1], 64)))
            if len(pending) == 2 or (dy, dx) == (2, 2):
                slot = pending[0][0] % 4 // 2
                first = pending[0][1]
                second = lane_roll(pending[-1][1], 64)
                turn_ref[slot, :, 0:64] = jnp.where(low, first, second).T
                for i, (row, _) in enumerate(pending):
                    for core in range(2):
                        at = 64 * i + 2 * core
                        even = turn_ref[slot, pl.ds(at, 16, stride=4), :]
                        odd = turn_ref[slot, pl.ds(at + 1, 16, stride=4), :]
                        out_ref[dz, core, pl.ds(row, 16, stride=16), :] = jnp.where(
                            low16, even, lane_roll(odd, 64)
                        )
                pending = []


def decoder_rows(dec_ref, local_ref):
    even = dec_ref[pl.ds(0, 16, stride=2), :]
    odd = dec_ref[pl.ds(1, 16, stride=2), :]
    both = jnp.where(iota((16, 128), 1) < 64, even, odd)
    for g, rows in ((0, jnp.zeros((7, 128), F32)), (1, both[0:7]), (2, both[7:14])):
        for core in range(2):
            for k in range(16):
                local_ref[g, core, 16 * k + 9 : 16 * k + 16, :] = rows


def step_kernel(
    coords, links, feat_hbm, target_hbm, cw_ref, dw_ref,
    out_ref, coarse_ref, dec_out,
    wide_ref, wdec_ref, target_ref, feat_ref, pooled_ref, spot_out, spot_in, plane_ref, sib_in, sib_ref, band_ref, frame_ref, pre_ref, up_ref, mixed_ref,
    bandt_ref, bandb_ref, tiles_ref, part_ref, edge_out, edge_in, cot_out, cot_in, spot_ref, sum_ref,
    cot_ref, res_ref, ext_ref, taps_ref, cat_ref, dcross_ref, halo_ref, rim_ref, line_ref, full_ref, lhs_ref, high_ref,
    low_ref, dpre_ref, cross_ref, turn_ref, dec_ref, local_ref, mate_ref, half_ref, chips_ref, parts_ref,
    target_sem, feat_sems, spot_sems, sib_sems, edge_sends, edge_recvs, cot_sends, cot_recvs, mate_sends, mate_recvs,
    chip_sends, chip_recvs, dp_sends, dp_recvs,
):
    slab, dp = lax.axis_index("slab"), lax.axis_index("dp")
    count = lax.axis_size("slab")
    core, chip = slab % 2, slab // 2
    chips, copies = count // 2, lax.axis_size("dp")
    meta = Meta(coords, links, slab, count)
    sibling = {"slab": slab + 1 - 2 * core}
    around = [{"slab": lax.rem(slab + 1, count)}, {"slab": lax.rem(slab + count - 1, count)}]

    def peer(r):
        return lax.rem(chip + r, chips)

    def twin(r):
        return lax.rem(dp + r, copies)

    def remote(src, dst, send, recv, device):
        return pltpu.make_async_remote_copy(
            src_ref=src,
            dst_ref=dst,
            send_sem=send,
            recv_sem=recv,
            device_id=device,
            device_id_type=pl.DeviceIdType.MESH,
        )

    barrier = pltpu.get_barrier_semaphore()
    greeted = around + [{"slab": 2 * peer(r) + core} for r in range(1, chips)]
    greeted = greeted + [{"dp": twin(r)} for r in range(1, copies)]
    for device in greeted:
        pl.semaphore_signal(barrier, inc=1, device_id=device, device_id_type=pl.DeviceIdType.MESH)

    loads = [
        pltpu.make_async_copy(feat_hbm.at[b], feat_ref.at[b], feat_sems.at[b]) for b in range(B)
    ]
    for load in loads:
        load.start()
    measured = pltpu.make_async_copy(target_hbm, target_ref, target_sem.at[0])
    measured.start()
    widen_weights(cw_ref, dw_ref, wide_ref, wdec_ref)
    coarse_weights(wide_ref, band_ref)
    pool_phase(feat_ref, pooled_ref, loads)
    line = iota((2 * B, 128), 0)
    spots = jnp.zeros((2 * B, 128), jnp.int32)
    for b in range(B):
        for i in range(2):
            spots = jnp.where(line == B * i + b, meta[b, i], spots)
    spot_out[...] = spots
    plane_ref[...] = pooled_ref[7 * (1 - core)].astype(BF16)
    pl.semaphore_wait(barrier, len(greeted))
    swap = remote(plane_ref, sib_in, sib_sems.at[0], sib_sems.at[1], sibling)
    swap.start()
    places = remote(spot_out, spot_in, spot_sems.at[0], spot_sems.at[1], sibling)
    places.start()
    frame_coarse(meta, pooled_ref, frame_ref)
    spread_weights(wdec_ref, high_ref, low_ref)
    decoder_bands(wdec_ref, bandt_ref)
    bandb_ref[...] = bandt_ref[...].astype(BF16)
    swap.wait()
    places.wait()
    sib_ref[...] = sib_in[...].astype(F32)
    frame_sibling(meta, spot_in[...], sib_ref, frame_ref, core)
    coarse_conv(frame_ref, band_ref, pre_ref)

    mix_phase(meta, feat_ref, pre_ref, up_ref, mixed_ref, [0, 7])
    edge_phase(mixed_ref, bandb_ref, edge_out)
    edges = [
        remote(edge_out.at[i], edge_in.at[i], edge_sends.at[i], edge_recvs.at[i], around[i])
        for i in range(2)
    ]
    for copy in edges:
        copy.start()
    mix_phase(meta, feat_ref, pre_ref, up_ref, mixed_ref, [1, 2, 3, 4, 5, 6])
    decode_phase(mixed_ref, bandb_ref, tiles_ref, part_ref)
    measured.wait()
    target_phase(target_ref, spot_ref)
    inner = (1, 14, 7)
    predict_y(meta, part_ref, halo_ref, sum_ref, inner)
    for copy in edges:
        copy.wait()
    receive_edges(meta, part_ref, edge_in)
    predict_y(meta, part_ref, halo_ref, sum_ref, [0, 15])
    predict_x(meta, sum_ref, spot_ref, res_ref, cot_ref, [0, 15])
    extend_phase(meta, cot_ref, ext_ref, full_ref, [0, 15])
    extend_rows(meta, ext_ref, [(1, 1), (16, 1)])
    for b in range(B):
        cot_out[0, b] = ext_ref[tall_at(b, 16, 0, 32), :].astype(BF16)
        cot_out[1, b] = ext_ref[tall_at(b, 1, 0, 32), :].astype(BF16)
    sides = [
        remote(cot_out.at[i], cot_in.at[i], cot_sends.at[i], cot_recvs.at[i], around[i])
        for i in range(2)
    ]
    for copy in sides:
        copy.start()
    predict_x(meta, sum_ref, spot_ref, res_ref, cot_ref, inner)
    extend_phase(meta, cot_ref, ext_ref, full_ref, inner)
    full_rows(meta, cot_ref, halo_ref, full_ref)
    spread_gather(full_ref, lhs_ref, list(range(1, 17)))
    extend_rows(meta, ext_ref, [(2, 14)])
    adjoint_taps(ext_ref, taps_ref, (1, 16, 8))
    adjoint_place(taps_ref, cat_ref, inner)
    for copy in sides:
        copy.wait()
    full_edges(meta, cot_in, rim_ref, line_ref, full_ref)
    spread_gather(full_ref, lhs_ref, [0, 17])
    dpre_phase(meta, lhs_ref, high_ref, low_ref, pre_ref, dpre_ref)
    turned = turned_halves(dpre_ref)

    mates = [
        remote(local_ref.at[g, 1 - core], mate_ref.at[g], mate_sends.at[g], mate_recvs.at[g], sibling)
        for g in range(3)
    ]

    def to_chip(g, r):
        return remote(
            half_ref.at[g, peer(r)], chips_ref.at[g, chip],
            chip_sends.at[g, r], chip_recvs.at[g, chip], {"slab": 2 * peer(r) + core},
        )

    def from_chip(g, r):
        return remote(
            half_ref.at[g, chip], chips_ref.at[g, peer(r)],
            chip_sends.at[g, r], chip_recvs.at[g, peer(r)], {"slab": 2 * peer(r) + core},
        )

    def send_out(g):
        mates[g].wait_recv()
        half_ref[g] = (local_ref[g, core] + mate_ref[g]).reshape(chips, 16, 128)
        for r in range(1, chips):
            to_chip(g, r).start()
        chips_ref[g, chip] = half_ref[g, chip]

    def collect(g):
        for r in range(1, chips):
            from_chip(g, r).wait_recv()
        total = chips_ref[g, 0]
        for k in range(1, chips):
            total = total + chips_ref[g, k]
        parts_ref[dp, 16 * g : 16 * g + 16, :] = total

    for b in range(B):
        for i, z in ((0, 0), (1, 17)):
            got = pick(meta[b, 4 + i], range(B), lambda a: cot_in[i, a].astype(F32))
            ext_ref[tall_at(b, z, 0, 32), :] = got
    adjoint_taps(ext_ref, taps_ref, [0, 17])
    adjoint_place(taps_ref, cat_ref, [0, 15])
    decoder_grad(cat_ref, mixed_ref, dcross_ref, dec_ref)
    decoder_rows(dec_ref, local_ref)
    for g in range(3):
        coarse_grad(turned, frame_ref, cross_ref, turn_ref, local_ref, g)
        mates[g].start()
        if g > 0:
            send_out(g - 1)
    send_out(2)
    residual_out(res_ref, out_ref)
    for g in range(3):
        collect(g)

    def to_twin(r):
        return remote(
            parts_ref.at[dp], parts_ref.at[dp], dp_sends.at[r], dp_recvs.at[dp], {"dp": twin(r)}
        )

    def from_twin(r):
        return remote(
            parts_ref.at[dp], parts_ref.at[twin(r)], dp_sends.at[r], dp_recvs.at[twin(r)], {"dp": twin(r)}
        )

    for r in range(1, copies):
        to_twin(r).start()
    for r in range(1, copies):
        from_twin(r).wait_recv()
    total = parts_ref[0]
    for k in range(1, copies):
        total = total + parts_ref[k]
    for g in range(3):
        coarse_ref[9 * g : 9 * g + 9, :] = total[16 * g : 16 * g + 9]
    for tap in range(27):
        at = 25 + tap // 2 if tap < 14 else 41 + tap // 2 - 7
        dec_out[tap : tap + 1, :] = total[at : at + 1, 64 * (tap % 2) : 64 * (tap % 2) + 64]
    for g in range(3):
        mates[g].wait_send()
        for r in range(1, chips):
            to_chip(g, r).wait_send()
    for r in range(1, copies):
        to_twin(r).wait_send()


def hand_out(*refs):
    count = (len(refs) - 2) // 3
    ins, outs, held = refs[:count], refs[count : 2 * count], refs[2 * count : 3 * count]
    in_sems, out_sems = refs[3 * count :]
    loads = [pltpu.make_async_copy(ins[i], held[i], in_sems.at[i]) for i in range(count)]
    stores = [pltpu.make_async_copy(held[i], outs[i], out_sems.at[i]) for i in range(count)]
    for load in loads:
        load.start()
    for load, store in zip(loads, stores):
        load.wait()
        store.start()
    for store in stores:
        store.wait()


def shape(dims, dtype=F32):
    return jax.ShapeDtypeStruct(dims, dtype)


def per_device(features, target, block_coords, neighbours, owners, coarse_weight, decoder_weight):
    coords = block_coords[0, 0].T
    count, copies = lax.axis_size("slab"), lax.axis_size("dp")
    chips = count // 2
    scratch = [
        ((27 * 64, 128), F32),
        ((32, 128), F32),
        ((64, 256), F32),
        ((B, 16, 16, 1024), BF16),
        ((8, 32, 512), F32),
        ((2 * B, 128), jnp.int32),
        ((2 * B, 128), jnp.int32),
        ((32, 512), BF16),
        ((32, 512), BF16),
        ((32, 512), F32),
        ((9, 512, 256), BF16),
        ((3, 10, 32, 768), BF16),
        ((8, 32, 512), F32),
        ((32, 16, 128), F32),
        ((B, 16, 16, 1024), BF16),
        ((256, 1024), F32),
        ((256, 1024), BF16),
        ((16, 16, 256), F32),
        ((1024, 128), F32),
        ((2, B, 16, 128), F32),
        ((2, B, 16, 128), F32),
        ((2, B, 32, 128), BF16),
        ((2, B, 32, 128), BF16),
        ((1024, 128), F32),
        ((1024, 128), F32),
        ((1024, 128), F32),
        ((1024, 128), F32),
        ((B * 18 * 32, 128), F32),
        ((B, 18, 16, 128), F32),
        ((B, 16, 16, 256), BF16),
        ((256, 1024), F32),
        ((2 * B, 16, 128), F32),
        ((2, B, 16, 128), F32),
        ((4, 8 * B, 128), F32),
        ((B * 18 * 32, 128), F32),
        ((8, 32, 512), BF16),
        ((512, 512), BF16),
        ((512, 512), BF16),
        ((8, 32, 512), F32),
        ((3, 256, 512), F32),
        ((2, 128, 128), F32),
        ((32, 128), F32),
        ((3, 2, 256, 128), F32),
        ((3, 256, 128), F32),
        ((3, chips, 16, 128), F32),
        ((3, chips, 16, 128), F32),
        ((copies, 48, 128), F32),
    ]
    sems = [(1,), (B,), (2,), (2,), (2,), (2,), (2,), (2,), (3,), (3,), (3, chips), (3, chips), (copies,), (copies,)]
    outs = [shape((64, 256)), shape((27, 128)), shape((27, 64))]
    results = pl.pallas_call(
        step_kernel,
        in_specs=[SM] * 2 + [ANY] * 2 + [VM] * 2,
        out_shape=outs,
        out_specs=[VM, VM, VM],
        scratch_shapes=[pltpu.VMEM(d, t) for d, t in scratch]
        + [pltpu.SemaphoreType.DMA(d) for d in sems],
        compiler_params=pltpu.CompilerParams(
            collective_id=0, has_side_effects=True, vmem_limit_bytes=62 * 1024 * 1024
        ),
    )(
        coords, neighbours[0, 0], features[0, 0], target[0, 0].reshape(64, 256),
        coarse_weight, decoder_weight,
    )
    res, mine, dec = pl.pallas_call(
        hand_out,
        in_specs=[ANY] * 3,
        out_shape=outs,
        out_specs=[ANY] * 3,
        scratch_shapes=[pltpu.VMEM(out.shape, F32) for out in outs]
        + [pltpu.SemaphoreType.DMA((3,))] * 2,
    )(*results)
    return res.reshape(1, 1, B, 16, 256), mine, dec


def solution(mesh):
    placed = (
        P("dp", "slab", None, None, None, None),
        P("dp", "slab", None, None, None),
        P("dp", "slab", None, None),
        P("dp", "slab", None, None),
        P("dp", "slab", None, None),
        P(),
        P(),
    )
    return jax.shard_map(
        per_device,
        mesh=mesh,
        in_specs=placed,
        out_specs=(P("dp", "slab", None, None, None), P(None, "slab"), P()),
        check_vma=False,
    )
```

```python
import jax
import jax.numpy as jnp
from jax import lax
from jax.experimental import pallas as pl
from jax.experimental.pallas import tpu as pltpu
from jax.sharding import PartitionSpec as P

F32 = jnp.float32
BF16 = jnp.bfloat16
VM = pl.BlockSpec(memory_space=pltpu.VMEM)
SM = pl.BlockSpec(memory_space=pltpu.SMEM)
ANY = pl.BlockSpec(memory_space=pl.ANY)
B = 4


def iota(shape, dim):
    return lax.broadcasted_iota(jnp.int32, shape, dim)


def repeat(count, body, step):
    def some(i, unused):
        for k in range(step):
            body(i * step + k)
        return unused

    if step == count:
        some(0, 0)
    else:
        lax.fori_loop(0, count // step, some, 0)


def lane_roll(v, shift):
    return pltpu.roll(v, shift % 128, v.ndim - 1)


def group_at(dz, dy):
    if dz == 0:
        return 24 * dy
    if dz == 2:
        return 128 + 24 * dy
    return 72 + 24 * dy if dy < 2 else 128 + 72


class Meta:
    def __init__(self, coords, links, slab, count):
        self.coords, self.links = coords, links
        self.ends = {4: slab == 0, 5: slab == count - 1}

    def __getitem__(self, at):
        b, col = at
        if col < 4:
            return self.coords[col, b]
        link = self.links[b, col - 4]
        return jnp.where(self.ends[col], -1, link) if col in self.ends else link


def widen_weights(cw_ref, dw_ref, wide_ref, wdec_ref):
    low = iota((27, 128), 1) < 64
    for t in range(32):
        v = cw_ref[:, 128 * t : 128 * t + 128].astype(F32)
        turned = lane_roll(v, 64)
        wide_ref[pl.ds(2 * t, 27, stride=64), :] = jnp.where(low, v, turned)
        wide_ref[pl.ds(2 * t + 1, 27, stride=64), :] = jnp.where(low, turned, v)
    w = dw_ref[...].astype(F32)
    wdec_ref[...] = jnp.zeros_like(wdec_ref)
    wdec_ref[0:27, 0:64] = w
    wdec_ref[0:27, 64:128] = w


def pool_phase(feat_ref, pooled_ref, loads):
    row, col = iota((64, 256), 0), iota((64, 256), 1)
    hit = (row // 8 == col // 32) & (row % 8 == (col % 16) // 2)
    gather = jnp.where(hit, 0.125, 0.0).astype(BF16)
    low = iota((64, 128), 1) < 64
    for b in range(B):
        loads[b].wait()
        rows = jnp.dot(gather, feat_ref[b].reshape(256, 1024), preferred_element_type=F32)
        for p in range(4):
            first = rows[:, 256 * p : 256 * p + 128]
            second = rows[:, 256 * p + 128 : 256 * p + 256]
            both = jnp.where(low, first + lane_roll(first, 64), second + lane_roll(second, 64))
            both = both.astype(BF16).astype(F32)
            for z in range(8):
                pooled_ref[z, 8 * b : 8 * b + 8, 128 * p : 128 * p + 128] = both[8 * z : 8 * z + 8]


def coarse_weights(wide_ref, band_ref):
    low = iota((64, 128), 1) < 64
    zero = jnp.zeros((64, 128), F32)
    for k in range(9):
        taps = [wide_ref[64 * (3 * k + dx) : 64 * (3 * k + dx) + 64, :] for dx in range(3)]
        for t in range(2):
            for kx in range(8):
                d0 = kx - 1 - 2 * t
                d1 = d0 - 1
                v0 = taps[d0] if 0 <= d0 < 3 else zero
                v1 = taps[d1] if 0 <= d1 < 3 else zero
                band_ref[k, 64 * kx : 64 * kx + 64, 128 * t : 128 * t + 128] = jnp.where(
                    low, v0, v1
                ).astype(BF16)


def pick(link, slots, load):
    v = None
    for a in slots:
        hit = link == a if not isinstance(link, list) else link[a]
        got = load(a)
        v = jnp.where(hit, got, jnp.zeros_like(got) if v is None else v)
    return v


def others(b):
    return [a for a in range(B) if a != b]


def framer(meta, spots=None):
    row = iota((8, 768), 0)

    def masked(cond, v):
        return jnp.where(cond, v, jnp.zeros_like(v))

    def roles(b):
        bx, by = meta[b, 0], meta[b, 1]
        found = {key: [] for key in ((0, 0), (0, 1), (1, 0), (1, 1))}
        for a in range(B):
            if spots is None:
                ax, ay = meta[a, 0], meta[a, 1]
            else:
                ax, ay = (
                    jnp.broadcast_to(spots[B * i + a : B * i + a + 1, :], (8, 128)) for i in range(2)
                )
            same = (ax >= 0) & (bx >= 0) & ((ax >> 1) == (bx >> 1)) & ((ay >> 1) == (by >> 1))
            for key in found:
                off_x = ax != bx if key[0] else ax == bx
                off_y = ay != by if key[1] else ay == by
                found[key].append(same & off_x & off_y)
        return found

    def rows_of(view, who, b):
        xh, yh = meta[b, 0] & 1, meta[b, 1] & 1

        def take(key, lo, hi):
            if spots is None:
                slots = [b] if key == (0, 0) else others(b)
                return pick(who[key], slots, lambda a: view(slice(8 * a, 8 * a + 8), slice(lo, hi)))
            parts = [
                pick(who[key], range(B), lambda a: view(slice(8 * a, 8 * a + 8), slice(at, at + 128)))
                for at in range(lo, hi, 128)
            ]
            return parts[0] if len(parts) == 1 else jnp.concatenate(parts, axis=1)

        def wide(mid, side):
            return jnp.concatenate(
                [
                    masked(xh == 1, take(side, 384, 512)),
                    take(mid, 0, 512),
                    masked(xh == 0, take(side, 0, 128)),
                ],
                axis=1,
            )

        own = wide((0, 0), (1, 0))
        near = wide((0, 1), (1, 1))
        before = jnp.where(row == 0, masked(yh == 1, pltpu.roll(near, 1, 0)), pltpu.roll(own, 1, 0))
        after = jnp.where(row == 7, masked(yh == 0, pltpu.roll(near, 7, 0)), pltpu.roll(own, 7, 0))
        return before, own, after

    return masked, [roles(b) for b in range(B)], rows_of


def frame_coarse(meta, pooled_ref, frame_ref):
    masked, roles, rows_of = framer(meta)

    def one_plane(z):
        for q in range(2):
            pair = [rows_of(lambda r, c: pooled_ref[z, r, c], roles[b], b) for b in (2 * q, 2 * q + 1)]
            for dy in range(3):
                frame_ref[dy, z + 1, 16 * q : 16 * q + 16, :] = jnp.concatenate(
                    [pair[0][dy], pair[1][dy]], axis=0
                ).astype(BF16)

    repeat(8, one_plane, 4)


def frame_sibling(meta, spots, sib_ref, frame_ref, zh):
    masked, roles, rows_of = framer(meta, spots)
    for q in range(2):
        pair = [rows_of(lambda r, c: sib_ref[r, c], roles[b], b) for b in (2 * q, 2 * q + 1)]
        for dy in range(3):
            both = jnp.concatenate([pair[0][dy], pair[1][dy]], axis=0)
            frame_ref[dy, 0, 16 * q : 16 * q + 16, :] = masked(zh == 1, both).astype(BF16)
            frame_ref[dy, 9, 16 * q : 16 * q + 16, :] = masked(zh == 0, both).astype(BF16)


def coarse_conv(frame_ref, band_ref, pre_ref):
    for h in range(2):
        total = None
        for dz in range(3):
            for dy in range(3):
                lhs = frame_ref[dy, dz : dz + 8, :, 256 * h : 256 * h + 512].reshape(256, 512)
                term = jnp.dot(lhs, band_ref[3 * dz + dy], preferred_element_type=F32)
                total = term if total is None else total + term
        pre_ref[:, :, 256 * h : 256 * h + 256] = total.reshape(8, 32, 256)


def mix_phase(meta, feat_ref, pre_ref, up_ref, mixed_ref, planes):
    low = iota((8, 128), 1) < 64

    def one(zc):
        for b in range(B):
            alive = meta[b, 0] >= 0
            for p in range(4):
                v = pre_ref[zc, 8 * b : 8 * b + 8, 128 * p : 128 * p + 128]
                v = jnp.maximum(v, 0.0).astype(BF16).astype(F32)
                turned = lane_roll(v, 64)
                for half in range(2):
                    d = jnp.where(low, v, turned) if half == 0 else jnp.where(low, turned, v)
                    for r in range(2):
                        up_ref[8 * b + 2 * p + half, pl.ds(r, 8, stride=2), :] = d
            for l in range(8):
                u = up_ref[8 * b + l]
                for r in range(2):
                    f = feat_ref[b, 2 * zc + r, :, 128 * l : 128 * l + 128].astype(F32)
                    m = jnp.where(alive, f + u, 0.0)
                    mixed_ref[b, 2 * zc + r, :, 128 * l : 128 * l + 128] = m.astype(BF16)

    for zc in planes:
        one(zc)


def decoder_bands(wdec_ref, bandt_ref):
    xi = iota((24, 128), 0)
    half = iota((24, 128), 1) // 64
    bandt_ref[...] = jnp.zeros_like(bandt_ref)
    for dz in range(3):
        for dy in range(3):
            taps = [
                jnp.broadcast_to(wdec_ref[9 * dz + 3 * dy + dx : 9 * dz + 3 * dy + dx + 1, :], (24, 128))
                for dx in range(3)
            ]
            at = group_at(dz, dy)
            for l in range(8):
                x = 2 * l + half
                v = jnp.zeros((24, 128), F32)
                for dx in range(3):
                    v = jnp.where(xi == x - dx + 2, taps[dx], v)
                bandt_ref[at : at + 24, 128 * l : 128 * l + 128] = v


def edge_phase(mixed_ref, bandb_ref, edge_ref):
    for side, z, at in ((0, 15, 0), (1, 0, 128)):
        edge = lax.dot_general(
            mixed_ref[:, z].reshape(64, 1024),
            bandb_ref[at : at + 128, :],
            (((1,), (1,)), ((), ())),
            preferred_element_type=F32,
        )
        edge_ref[side] = edge.reshape(B, 16, 128)


def decode_phase(mixed_ref, bandb_ref, tiles_ref, part_ref):
    lane = iota((16, 128), 1)
    bandt = bandb_ref[...]
    for b in range(B):
        tiles = lax.dot_general(
            mixed_ref[b].reshape(256, 1024),
            bandt,
            (((1,), (1,)), ((), ())),
            preferred_element_type=F32,
        )
        tiles_ref[...] = tiles.reshape(16, 16, 256)
        for z in range(16):
            t0, t1 = tiles_ref[z, :, 0:128], tiles_ref[z, :, 128:256]
            v = jnp.where(lane < 48, lane_roll(t0, -72), lane_roll(t1, -24))
            if z > 0:
                v = v + tiles_ref[z - 1, :, 0:128]
            if z < 15:
                v = v + tiles_ref[z + 1, :, 128:256]
            part_ref[256 * b + 16 * z : 256 * b + 16 * z + 16, :] = v


def target_phase(target_ref, wide_ref):
    for y in range(16):
        j, k = y // 8, y % 8
        v = target_ref[:, 128 * j : 128 * j + 128]
        wide_ref[pl.ds(y, 64, stride=16), :] = lane_roll(v, 1 - 16 * k)


def each(planes, body):
    if isinstance(planes, list):
        for z in planes:
            body(z)
    else:
        first, count, step = planes
        repeat(count, lambda i: body(first + i), step)


def plane_at(b, z):
    at = 256 * b + 16 * z
    return pl.ds(at if isinstance(at, int) else pl.multiple_of(at, 16), 16)


def tall_at(b, z, row, rows):
    at = 32 * (18 * b + z) + row
    return pl.ds(at if isinstance(at, int) else pl.multiple_of(at, 8), rows)


def receive_edges(meta, part_ref, edge_ref):
    for b in range(B):
        for i, z in ((0, 0), (1, 15)):
            got = pick(meta[b, 4 + i], range(B), lambda a: edge_ref[i, a])
            part_ref[plane_at(b, z), :] = part_ref[plane_at(b, z), :] + got


def predict_y(meta, part_ref, halo_ref, sum_ref, planes):
    row = iota((16, 128), 0)
    for b in range(B):
        for i, y in ((0, 15), (1, 0)):
            halo_ref[2 * b + i] = pick(
                meta[b, 6 + i], others(b), lambda a: part_ref[pl.ds(256 * a + y, 16, stride=16), :]
            )
    for b in range(B):

        def along_y(z, b=b):
            own = part_ref[plane_at(b, z), :]
            low = jnp.broadcast_to(halo_ref[2 * b, pl.ds(z, 1), :], (16, 128))
            high = jnp.broadcast_to(halo_ref[2 * b + 1, pl.ds(z, 1), :], (16, 128))
            d0 = jnp.where(row == 0, low, pltpu.roll(own, 1, 0))
            d2 = jnp.where(row == 15, high, pltpu.roll(own, 15, 0))
            sum_ref[plane_at(b, z), :] = d0 + lane_roll(own, -24) + lane_roll(d2, -48)

        each(planes, along_y)


def predict_x(meta, sum_ref, wide_ref, res_ref, cot_ref, planes):
    lane = iota((16, 128), 1)
    for b in range(B):

        def along_x(z, b=b):
            at = plane_at(b, z)
            own = sum_ref[at, :]
            low, high = (
                pick(meta[b, 8 + i], others(b), lambda a: sum_ref[plane_at(a, z), :]) for i in range(2)
            )
            own = own + jnp.where(lane == 1, lane_roll(low, -16), 0.0)
            own = own + jnp.where(lane == 16, lane_roll(high, 16), 0.0)
            keep = (lane >= 1) & (lane <= 16) & (meta[b, 0] >= 0)
            res = jnp.where(keep, own - wide_ref[at, :], 0.0)
            res_ref[at, :] = res
            cot_ref[at, :] = (res * (1.0 / 16384)).astype(BF16).astype(F32)

        each(planes, along_x)


def residual_out(res_ref, out_ref):
    group = iota((64, 128), 1) // 16
    for j in range(2):
        v = jnp.zeros((64, 128), F32)
        for k in range(8):
            got = lane_roll(res_ref[pl.ds(8 * j + k, 64, stride=16), :], 16 * k - 1)
            v = jnp.where(group == k, got, v)
        out_ref[:, 128 * j : 128 * j + 128] = v


def spread_x(own, low, high):
    lane = iota(own.shape, 1)
    own = jnp.where(lane == 0, lane_roll(low, -16), own)
    return jnp.where(lane == 17, lane_roll(high, 16), own)


def sides_of(meta, b, load):
    return load(b), *(pick(meta[b, 8 + i], others(b), load) for i in range(2))


ROWS = ((0, 7, 23, 15), (1, 24, 8, 0))


def extend_phase(meta, cot_ref, ext_ref, full_ref, planes):
    for b in range(B):

        def along_x(z, b=b):
            v = spread_x(*sides_of(meta, b, lambda a: cot_ref[plane_at(a, z), :]))
            ext_ref[tall_at(b, z + 1, 8, 16), :] = v
            full_ref[tall_at(b, z + 1, 8, 16), :] = v

        each(planes, along_x)


def extend_rows(meta, ext_ref, spans):
    for b in range(B):
        for i, row, source, _ in ROWS:
            for z, count in spans:
                ext_ref[pl.ds(32 * (18 * b + z) + row, count, stride=32), :] = pick(
                    meta[b, 6 + i],
                    others(b),
                    lambda a: ext_ref[pl.ds(32 * (18 * a + z) + source, count, stride=32), :],
                )


def full_rows(meta, cot_ref, halo_ref, full_ref):
    for b in range(B):
        for i, _, _, y in ROWS:
            halo_ref[2 * b + i] = pick(
                meta[b, 6 + i], others(b), lambda a: cot_ref[pl.ds(256 * a + y, 16, stride=16), :]
            )
    for b in range(B):
        for i, row, _, _ in ROWS:
            v = spread_x(*sides_of(meta, b, lambda a: halo_ref[2 * a + i]))
            full_ref[pl.ds(32 * (18 * b + 1) + row, 16, stride=32), :] = v


def full_edges(meta, cot_in, rim_ref, line_ref, full_ref):
    lane = iota((16, 128), 1)
    for b in range(B):
        for i in range(2):
            got = pick(meta[b, 4 + i], range(B), lambda a: cot_in[i, a].astype(F32))[8:24]
            rim_ref[i, b] = jnp.where((lane >= 1) & (lane <= 16), got, 0.0)
    for b in range(B):
        for i, z in ((0, 0), (1, 17)):
            v = spread_x(*sides_of(meta, b, lambda a: rim_ref[i, a]))
            full_ref[tall_at(b, z, 8, 16), :] = v
            for k, _, _, y in ROWS:
                line_ref[2 * i + k, 8 * b : 8 * b + 8, :] = jnp.broadcast_to(
                    pick(meta[b, 6 + k], others(b), lambda a: rim_ref[i, a, y : y + 1, :]), (8, 128)
                )
    for b in range(B):
        for i, z in ((0, 0), (1, 17)):
            for k, row, _, _ in ROWS:
                v = spread_x(*sides_of(meta, b, lambda a: line_ref[2 * i + k, 8 * a : 8 * a + 8, :]))
                full_ref[tall_at(b, z, row, 1), :] = v[0:1]


def adjoint_taps(ext_ref, taps_ref, planes):
    lane = iota((16, 128), 1)
    for b in range(B):

        def gather(z, b=b):
            s0, s1, s2 = (ext_ref[pl.ds(32 * (18 * b + z) + 9 - dy, 16), :] for dy in range(3))
            taps_ref[b, z] = jnp.where(
                lane < 24, s0, jnp.where(lane < 48, lane_roll(s1, 24), lane_roll(s2, 48))
            )

        each(planes, gather)


def adjoint_place(taps_ref, cat_ref, planes):
    lane = iota((16, 128), 1)
    for b in range(B):

        def place(z, b=b):
            mid = taps_ref[b, z + 1]
            t0 = jnp.where(lane < 72, taps_ref[b, z + 2], lane_roll(mid, 72))
            t1 = jnp.where(lane < 72, taps_ref[b, z], lane_roll(mid, 24))
            cat_ref[b, z] = jnp.concatenate([t0, t1], axis=1).astype(BF16)

        each(planes, place)


def decoder_grad(cat_ref, mixed_ref, cross_ref, out_ref):
    cross_ref[...] = lax.dot_general(
        cat_ref[...].reshape(1024, 256),
        mixed_ref[...].reshape(1024, 1024),
        (((0,), (0,)), ((), ())),
        preferred_element_type=F32,
    )
    xi = iota((24, 128), 0)
    half = iota((24, 128), 1) // 64
    for dz in range(3):
        for dy in range(3):
            at = group_at(dz, dy)
            sums = [jnp.zeros((24, 128), F32) for _ in range(3)]
            for l in range(8):
                v = cross_ref[at : at + 24, 128 * l : 128 * l + 128]
                for dx in range(3):
                    sums[dx] = sums[dx] + jnp.where(xi == 2 * l + half - dx + 2, v, 0.0)
            for dx in range(3):
                line = jnp.sum(sums[dx], axis=0, keepdims=True)
                line = line + lane_roll(line, 64)
                tap = 9 * dz + 3 * dy + dx
                out_ref[tap : tap + 1, :] = line


def spread_gather(full_ref, lhs_ref, planes):
    group = iota((8, 128), 1) // 32
    for z in planes:
        got = []
        for b in range(B):
            v = full_ref[pl.ds(32 * (18 * b + z) + 7, 8, stride=2), :]
            for j in range(1, 4):
                turned = lane_roll(full_ref[pl.ds(32 * (18 * b + z) + 7 + j, 8, stride=2), :], 32 * j)
                v = jnp.where(group == j, turned, v)
            got.append(v)
        p = jnp.concatenate(got, axis=0).astype(BF16)
        for i in range(z % 2, 4, 2):
            zc = (z - i) // 2
            if 0 <= zc < 8:
                lhs_ref[zc, :, 128 * i : 128 * i + 128] = p


def spread_weights(wdec_ref, high_ref, low_ref):
    row, col = iota((64, 32), 0), iota((64, 32), 1)

    def pick(k, d):
        return ((k == 2 - d) | (k == 3 - d)).astype(F32)

    sel = pick(row // 16, col // 9) * pick((row // 4) % 4, (col // 3) % 3) * pick(row % 4, col % 3)
    sel = jnp.where(col < 27, sel, 0.0).astype(BF16)
    summed = jnp.dot(sel, wdec_ref[...].astype(BF16), preferred_element_type=F32)
    x = iota((32, 128), 0)
    half = iota((32, 128), 1) // 64
    for ij in range(16):
        taps = [jnp.broadcast_to(summed[4 * ij + k : 4 * ij + k + 1, :], (32, 128)) for k in range(4)]
        for t in range(4):
            v = jnp.zeros((32, 128), F32)
            for k in range(4):
                v = jnp.where(x - 2 * (2 * t + half) == k, taps[k], v)
            hi = v.astype(BF16)
            high_ref[32 * ij : 32 * ij + 32, 128 * t : 128 * t + 128] = hi
            low_ref[32 * ij : 32 * ij + 32, 128 * t : 128 * t + 128] = (v - hi.astype(F32)).astype(BF16)


def dpre_phase(meta, lhs_ref, high_ref, low_ref, pre_ref, dpre_ref):
    lhs = lhs_ref[...].reshape(256, 512)
    up = jnp.dot(lhs, high_ref[...], preferred_element_type=F32)
    up = up + jnp.dot(lhs, low_ref[...], preferred_element_type=F32)
    up = up.astype(BF16).astype(F32).reshape(8, 32, 512)
    for b in range(B):
        mine = up[:, 8 * b : 8 * b + 8]
        keep = (pre_ref[:, 8 * b : 8 * b + 8] > 0) & (meta[b, 0] >= 0)
        dpre_ref[:, 8 * b : 8 * b + 8] = jnp.where(keep, mine, 0.0)


def turned_halves(dpre_ref):
    dpre = dpre_ref[...].reshape(256, 512)
    return [dpre[:, 256 * h : 256 * h + 256].T.astype(BF16) for h in range(2)]


def coarse_grad(turned, frame_ref, cross_ref, turn_ref, out_ref, dz):
    low = iota((64, 128), 1) < 64
    low16 = iota((16, 128), 1) < 64
    pending = []
    for dy in range(3):
        total = None
        for h in range(2):
            rhs = frame_ref[dy, dz : dz + 8, :, 256 * h : 256 * h + 512].reshape(256, 512)
            term = jnp.dot(turned[h], rhs, preferred_element_type=F32)
            total = term if total is None else total + term
        cross_ref[dy] = total
        for dx in range(3):
            sums = [None, None]
            for n in range(4):
                m = n + dx + 1
                v = cross_ref[dy, 64 * n : 64 * n + 64, 128 * (m // 2) : 128 * (m // 2) + 128]
                sums[m % 2] = v if sums[m % 2] is None else sums[m % 2] + v
            pending.append((3 * dy + dx, sums[0] + lane_roll(sums[1], 64)))
            if len(pending) == 2 or (dy, dx) == (2, 2):
                slot = pending[0][0] % 4 // 2
                first = pending[0][1]
                second = lane_roll(pending[-1][1], 64)
                turn_ref[slot, :, 0:64] = jnp.where(low, first, second).T
                for i, (row, _) in enumerate(pending):
                    for core in range(2):
                        at = 64 * i + 2 * core
                        even = turn_ref[slot, pl.ds(at, 16, stride=4), :]
                        odd = turn_ref[slot, pl.ds(at + 1, 16, stride=4), :]
                        out_ref[dz, core, pl.ds(row, 16, stride=16), :] = jnp.where(
                            low16, even, lane_roll(odd, 64)
                        )
                pending = []


def decoder_rows(dec_ref, local_ref):
    even = dec_ref[pl.ds(0, 16, stride=2), :]
    odd = dec_ref[pl.ds(1, 16, stride=2), :]
    both = jnp.where(iota((16, 128), 1) < 64, even, odd)
    for g, rows in ((0, jnp.zeros((7, 128), F32)), (1, both[0:7]), (2, both[7:14])):
        for core in range(2):
            for k in range(16):
                local_ref[g, core, 16 * k + 9 : 16 * k + 16, :] = rows


def step_kernel(
    coords, links, feat_hbm, target_hbm, cw_ref, dw_ref,
    out_ref, coarse_ref, dec_out,
    wide_ref, wdec_ref, target_ref, feat_ref, pooled_ref, spot_out, spot_in, plane_ref, sib_in, sib_ref, band_ref, frame_ref, pre_ref, up_ref, mixed_ref,
    bandt_ref, bandb_ref, tiles_ref, part_ref, edge_out, edge_in, cot_out, cot_in, spot_ref, sum_ref,
    cot_ref, res_ref, ext_ref, taps_ref, cat_ref, dcross_ref, halo_ref, rim_ref, line_ref, full_ref, lhs_ref, high_ref,
    low_ref, dpre_ref, cross_ref, turn_ref, dec_ref, local_ref, mate_ref, half_ref, chips_ref, parts_ref,
    target_sem, feat_sems, spot_sems, sib_sems, edge_sends, edge_recvs, cot_sends, cot_recvs, mate_sends, mate_recvs,
    chip_sends, chip_recvs, dp_sends, dp_recvs,
):
    slab, dp = lax.axis_index("slab"), lax.axis_index("dp")
    count = lax.axis_size("slab")
    core, chip = slab % 2, slab // 2
    chips, copies = count // 2, lax.axis_size("dp")
    meta = Meta(coords, links, slab, count)
    sibling = {"slab": slab + 1 - 2 * core}
    around = [{"slab": lax.rem(slab + 1, count)}, {"slab": lax.rem(slab + count - 1, count)}]

    def peer(r):
        return lax.rem(chip + r, chips)

    def twin(r):
        return lax.rem(dp + r, copies)

    def remote(src, dst, send, recv, device):
        return pltpu.make_async_remote_copy(
            src_ref=src,
            dst_ref=dst,
            send_sem=send,
            recv_sem=recv,
            device_id=device,
            device_id_type=pl.DeviceIdType.MESH,
        )

    barrier = pltpu.get_barrier_semaphore()
    greeted = around + [{"slab": 2 * peer(r) + core} for r in range(1, chips)]
    greeted = greeted + [{"dp": twin(r)} for r in range(1, copies)]
    for device in greeted:
        pl.semaphore_signal(barrier, inc=1, device_id=device, device_id_type=pl.DeviceIdType.MESH)

    loads = [
        pltpu.make_async_copy(feat_hbm.at[b], feat_ref.at[b], feat_sems.at[b]) for b in range(B)
    ]
    for load in loads:
        load.start()
    measured = pltpu.make_async_copy(target_hbm, target_ref, target_sem.at[0])
    measured.start()
    widen_weights(cw_ref, dw_ref, wide_ref, wdec_ref)
    coarse_weights(wide_ref, band_ref)
    pool_phase(feat_ref, pooled_ref, loads)
    line = iota((2 * B, 128), 0)
    spots = jnp.zeros((2 * B, 128), jnp.int32)
    for b in range(B):
        for i in range(2):
            spots = jnp.where(line == B * i + b, meta[b, i], spots)
    spot_out[...] = spots
    plane_ref[...] = pooled_ref[7 * (1 - core)].astype(BF16)
    pl.semaphore_wait(barrier, len(greeted))
    swap = remote(plane_ref, sib_in, sib_sems.at[0], sib_sems.at[1], sibling)
    swap.start()
    places = remote(spot_out, spot_in, spot_sems.at[0], spot_sems.at[1], sibling)
    places.start()
    frame_coarse(meta, pooled_ref, frame_ref)
    spread_weights(wdec_ref, high_ref, low_ref)
    decoder_bands(wdec_ref, bandt_ref)
    bandb_ref[...] = bandt_ref[...].astype(BF16)
    swap.wait()
    places.wait()
    sib_ref[...] = sib_in[...].astype(F32)
    frame_sibling(meta, spot_in[...], sib_ref, frame_ref, core)
    coarse_conv(frame_ref, band_ref, pre_ref)

    mix_phase(meta, feat_ref, pre_ref, up_ref, mixed_ref, [0, 7])
    edge_phase(mixed_ref, bandb_ref, edge_out)
    edges = [
        remote(edge_out.at[i], edge_in.at[i], edge_sends.at[i], edge_recvs.at[i], around[i])
        for i in range(2)
    ]
    for copy in edges:
        copy.start()
    mix_phase(meta, feat_ref, pre_ref, up_ref, mixed_ref, [1, 2, 3, 4, 5, 6])
    decode_phase(mixed_ref, bandb_ref, tiles_ref, part_ref)
    measured.wait()
    target_phase(target_ref, spot_ref)
    inner = (1, 14, 14)
    predict_y(meta, part_ref, halo_ref, sum_ref, inner)
    for copy in edges:
        copy.wait()
    receive_edges(meta, part_ref, edge_in)
    predict_y(meta, part_ref, halo_ref, sum_ref, [0, 15])
    predict_x(meta, sum_ref, spot_ref, res_ref, cot_ref, [0, 15])
    extend_phase(meta, cot_ref, ext_ref, full_ref, [0, 15])
    extend_rows(meta, ext_ref, [(1, 1), (16, 1)])
    for b in range(B):
        cot_out[0, b] = ext_ref[tall_at(b, 16, 0, 32), :].astype(BF16)
        cot_out[1, b] = ext_ref[tall_at(b, 1, 0, 32), :].astype(BF16)
    sides = [
        remote(cot_out.at[i], cot_in.at[i], cot_sends.at[i], cot_recvs.at[i], around[i])
        for i in range(2)
    ]
    for copy in sides:
        copy.start()
    predict_x(meta, sum_ref, spot_ref, res_ref, cot_ref, inner)
    extend_phase(meta, cot_ref, ext_ref, full_ref, inner)
    full_rows(meta, cot_ref, halo_ref, full_ref)
    spread_gather(full_ref, lhs_ref, list(range(1, 17)))
    extend_rows(meta, ext_ref, [(2, 14)])
    adjoint_taps(ext_ref, taps_ref, (1, 16, 16))
    adjoint_place(taps_ref, cat_ref, inner)
    for copy in sides:
        copy.wait()
    full_edges(meta, cot_in, rim_ref, line_ref, full_ref)
    spread_gather(full_ref, lhs_ref, [0, 17])
    dpre_phase(meta, lhs_ref, high_ref, low_ref, pre_ref, dpre_ref)
    turned = turned_halves(dpre_ref)

    mates = [
        remote(local_ref.at[g, 1 - core], mate_ref.at[g], mate_sends.at[g], mate_recvs.at[g], sibling)
        for g in range(3)
    ]

    def to_chip(g, r):
        return remote(
            half_ref.at[g, peer(r)], chips_ref.at[g, chip],
            chip_sends.at[g, r], chip_recvs.at[g, chip], {"slab": 2 * peer(r) + core},
        )

    def from_chip(g, r):
        return remote(
            half_ref.at[g, chip], chips_ref.at[g, peer(r)],
            chip_sends.at[g, r], chip_recvs.at[g, peer(r)], {"slab": 2 * peer(r) + core},
        )

    def send_out(g):
        mates[g].wait_recv()
        half_ref[g] = (local_ref[g, core] + mate_ref[g]).reshape(chips, 16, 128)
        for r in range(1, chips):
            to_chip(g, r).start()
        chips_ref[g, chip] = half_ref[g, chip]

    def collect(g):
        for r in range(1, chips):
            from_chip(g, r).wait_recv()
        total = chips_ref[g, 0]
        for k in range(1, chips):
            total = total + chips_ref[g, k]
        parts_ref[dp, 16 * g : 16 * g + 16, :] = total

    for b in range(B):
        for i, z in ((0, 0), (1, 17)):
            got = pick(meta[b, 4 + i], range(B), lambda a: cot_in[i, a].astype(F32))
            ext_ref[tall_at(b, z, 0, 32), :] = got
    adjoint_taps(ext_ref, taps_ref, [0, 17])
    adjoint_place(taps_ref, cat_ref, [0, 15])
    decoder_grad(cat_ref, mixed_ref, dcross_ref, dec_ref)
    decoder_rows(dec_ref, local_ref)
    for g in range(3):
        coarse_grad(turned, frame_ref, cross_ref, turn_ref, local_ref, g)
        mates[g].start()
        if g > 0:
            send_out(g - 1)
    send_out(2)
    residual_out(res_ref, out_ref)
    for g in range(3):
        collect(g)

    def to_twin(r):
        return remote(
            parts_ref.at[dp], parts_ref.at[dp], dp_sends.at[r], dp_recvs.at[dp], {"dp": twin(r)}
        )

    def from_twin(r):
        return remote(
            parts_ref.at[dp], parts_ref.at[twin(r)], dp_sends.at[r], dp_recvs.at[twin(r)], {"dp": twin(r)}
        )

    for r in range(1, copies):
        to_twin(r).start()
    for r in range(1, copies):
        from_twin(r).wait_recv()
    total = parts_ref[0]
    for k in range(1, copies):
        total = total + parts_ref[k]
    for g in range(3):
        coarse_ref[9 * g : 9 * g + 9, :] = total[16 * g : 16 * g + 9]
    for tap in range(27):
        at = 25 + tap // 2 if tap < 14 else 41 + tap // 2 - 7
        dec_out[tap : tap + 1, :] = total[at : at + 1, 64 * (tap % 2) : 64 * (tap % 2) + 64]
    for g in range(3):
        mates[g].wait_send()
        for r in range(1, chips):
            to_chip(g, r).wait_send()
    for r in range(1, copies):
        to_twin(r).wait_send()


def hand_out(*refs):
    count = (len(refs) - 2) // 3
    ins, outs, held = refs[:count], refs[count : 2 * count], refs[2 * count : 3 * count]
    in_sems, out_sems = refs[3 * count :]
    loads = [pltpu.make_async_copy(ins[i], held[i], in_sems.at[i]) for i in range(count)]
    stores = [pltpu.make_async_copy(held[i], outs[i], out_sems.at[i]) for i in range(count)]
    for load in loads:
        load.start()
    for load, store in zip(loads, stores):
        load.wait()
        store.start()
    for store in stores:
        store.wait()


def shape(dims, dtype=F32):
    return jax.ShapeDtypeStruct(dims, dtype)


def per_device(features, target, block_coords, neighbours, owners, coarse_weight, decoder_weight):
    coords = block_coords[0, 0].T
    count, copies = lax.axis_size("slab"), lax.axis_size("dp")
    chips = count // 2
    scratch = [
        ((27 * 64, 128), F32),
        ((32, 128), F32),
        ((64, 256), F32),
        ((B, 16, 16, 1024), BF16),
        ((8, 32, 512), F32),
        ((2 * B, 128), jnp.int32),
        ((2 * B, 128), jnp.int32),
        ((32, 512), BF16),
        ((32, 512), BF16),
        ((32, 512), F32),
        ((9, 512, 256), BF16),
        ((3, 10, 32, 768), BF16),
        ((8, 32, 512), F32),
        ((32, 16, 128), F32),
        ((B, 16, 16, 1024), BF16),
        ((256, 1024), F32),
        ((256, 1024), BF16),
        ((16, 16, 256), F32),
        ((1024, 128), F32),
        ((2, B, 16, 128), F32),
        ((2, B, 16, 128), F32),
        ((2, B, 32, 128), BF16),
        ((2, B, 32, 128), BF16),
        ((1024, 128), F32),
        ((1024, 128), F32),
        ((1024, 128), F32),
        ((1024, 128), F32),
        ((B * 18 * 32, 128), F32),
        ((B, 18, 16, 128), F32),
        ((B, 16, 16, 256), BF16),
        ((256, 1024), F32),
        ((2 * B, 16, 128), F32),
        ((2, B, 16, 128), F32),
        ((4, 8 * B, 128), F32),
        ((B * 18 * 32, 128), F32),
        ((8, 32, 512), BF16),
        ((512, 512), BF16),
        ((512, 512), BF16),
        ((8, 32, 512), F32),
        ((3, 256, 512), F32),
        ((2, 128, 128), F32),
        ((32, 128), F32),
        ((3, 2, 256, 128), F32),
        ((3, 256, 128), F32),
        ((3, chips, 16, 128), F32),
        ((3, chips, 16, 128), F32),
        ((copies, 48, 128), F32),
    ]
    sems = [(1,), (B,), (2,), (2,), (2,), (2,), (2,), (2,), (3,), (3,), (3, chips), (3, chips), (copies,), (copies,)]
    outs = [shape((64, 256)), shape((27, 128)), shape((27, 64))]
    results = pl.pallas_call(
        step_kernel,
        in_specs=[SM] * 2 + [ANY] * 2 + [VM] * 2,
        out_shape=outs,
        out_specs=[VM, VM, VM],
        scratch_shapes=[pltpu.VMEM(d, t) for d, t in scratch]
        + [pltpu.SemaphoreType.DMA(d) for d in sems],
        compiler_params=pltpu.CompilerParams(
            collective_id=0, has_side_effects=True, vmem_limit_bytes=62 * 1024 * 1024
        ),
    )(
        coords, neighbours[0, 0], features[0, 0], target[0, 0].reshape(64, 256),
        coarse_weight, decoder_weight,
    )
    res, mine, dec = pl.pallas_call(
        hand_out,
        in_specs=[ANY] * 3,
        out_shape=outs,
        out_specs=[ANY] * 3,
        scratch_shapes=[pltpu.VMEM(out.shape, F32) for out in outs]
        + [pltpu.SemaphoreType.DMA((3,))] * 2,
    )(*results)
    return res.reshape(1, 1, B, 16, 256), mine, dec


def solution(mesh):
    placed = (
        P("dp", "slab", None, None, None, None),
        P("dp", "slab", None, None, None),
        P("dp", "slab", None, None),
        P("dp", "slab", None, None),
        P("dp", "slab", None, None),
        P(),
        P(),
    )
    return jax.shard_map(
        per_device,
        mesh=mesh,
        in_specs=placed,
        out_specs=(P("dp", "slab", None, None, None), P(None, "slab"), P()),
        check_vma=False,
    )
```
